128 devices in a mesh: row: 16 (over x_lo, z, core), col: 8 (over x_hi, y).
Axes of the slice: x: 4 (x_hi: 2, x_lo: 2; x = x_hi * 2 + x_lo), y: 4, z: 4, core: 2. Of those that a mesh axis runs over, the one named last changes fastest.
Arguments:
- alignment_features: bfloat16 [512, 1024, 256], P('row', 'col'), may hold values from -6 to 6
- standardize_scale: float32 [256], replicated, may hold values from 0.5 to 1.5
- source_matrix: bfloat16 [256, 32], replicated, may hold values from -0.375 to 0.375
- target_matrix: bfloat16 [256, 32], replicated, may hold values from -0.375 to 0.375
- final_matrix: bfloat16 [1024, 128], replicated, may hold values from -3 to 3
- final_offset: float32 [128], replicated, may hold values from -4 to 4
Outputs:
- pair_update: bfloat16 [1024, 1024, 128], P('row', 'col')
The draws below stay inside these ranges and needn't reach their ends.
All inputs are finite; a program needn't handle non-finite values.
Results may differ from the reference program's by a relative error of at most 0.0054.
Values may be sent and summed in bfloat16 or wider, within the bound.
A program may use at most 64 MiB of HBM per device.

```python
import jax
import jax.numpy as jnp
from jax import lax

ALIGN_FEATURES = 256
HALF_WIDTH = 32
OUTC = 128
BLK = 16
AMINO_TOTAL = 1024
ALIGNED_TOTAL = 512


def level_of(stream_key, extent, cuts, smallest, largest):
    level = 1.0
    for axis_at, shards_of in cuts:
        heights = jax.random.uniform(jax.random.fold_in(jax.random.fold_in(stream_key, 6), axis_at), (shards_of,), jnp.float32, smallest / len(cuts), largest / len(cuts))
        level = level * jnp.repeat(jnp.exp(heights), extent[axis_at] // shards_of).reshape((-1,) + (1,) * (len(extent) - 1 - axis_at))
    return level


def bell_draw(own_key, extent, deviation, reach, cuts=(), held_as=jnp.bfloat16):
    factor_of = level_of(own_key, extent, cuts, -0.22, 0.18) if cuts else 1.0
    array = jax.random.normal(own_key, extent, jnp.float32) * deviation * factor_of
    return jnp.minimum(jnp.maximum(array, -reach), reach).astype(held_as)


def setup_inputs(seed: int = 0) -> dict:
    streams_of = jax.random.split(jax.random.key(seed), 7)
    alignment_features = bell_draw(streams_of[0], (ALIGNED_TOTAL, AMINO_TOTAL, ALIGN_FEATURES), 1.0, 6.0, ((0, 16), (1, 8)))
    standardize_scale = jnp.clip(jax.random.uniform(streams_of[1], (ALIGN_FEATURES,), jnp.float32, 0.5, 1.5), 0.5, 1.5)
    source_matrix = bell_draw(streams_of[2], (ALIGN_FEATURES, HALF_WIDTH), ALIGN_FEATURES ** -0.5, 0.375)
    target_matrix = bell_draw(streams_of[3], (ALIGN_FEATURES, HALF_WIDTH), ALIGN_FEATURES ** -0.5, 0.375)
    final_matrix = bell_draw(streams_of[4], (HALF_WIDTH * HALF_WIDTH, OUTC), 0.5, 3.0)
    final_offset = bell_draw(streams_of[5], (OUTC,), 1.0, 4.0, (), jnp.float32)
    return {"alignment_features": alignment_features, "standardize_scale": standardize_scale, "source_matrix": source_matrix, "target_matrix": target_matrix, "final_matrix": final_matrix, "final_offset": final_offset}


def reference(alignment_features, standardize_scale, source_matrix, target_matrix, final_matrix, final_offset):
    element_number = alignment_features.astype(jnp.float32)
    center = lax.optimization_barrier(jnp.mean(element_number, axis=-1, keepdims=True))
    spread = lax.optimization_barrier(jnp.mean(jnp.square(element_number - center), axis=-1, keepdims=True))
    standardized = ((element_number - center) * lax.rsqrt(spread + 1e-05) * standardize_scale).astype(jnp.bfloat16)
    unrolled_matrix = standardized.reshape(ALIGNED_TOTAL * AMINO_TOTAL, ALIGN_FEATURES)
    left = jnp.dot(unrolled_matrix, source_matrix, preferred_element_type=jnp.float32).astype(jnp.bfloat16).reshape(ALIGNED_TOTAL, AMINO_TOTAL, HALF_WIDTH)
    right = jnp.dot(unrolled_matrix, target_matrix, preferred_element_type=jnp.float32).astype(jnp.bfloat16).reshape(ALIGNED_TOTAL, AMINO_TOTAL, HALF_WIDTH)
    right_wide = right.astype(jnp.float32)
    weight_out = final_matrix.astype(jnp.float32).reshape(HALF_WIDTH, HALF_WIDTH, OUTC)
    blocks = jnp.moveaxis(left.reshape(ALIGNED_TOTAL, AMINO_TOTAL // BLK, BLK, HALF_WIDTH), 1, 0)

    def one_block(block):
        outer = jnp.einsum('sia,sjb->ijab', block.astype(jnp.float32), right_wide, precision=lax.Precision.HIGHEST) / ALIGNED_TOTAL
        outer = outer.astype(jnp.bfloat16).astype(jnp.float32)
        result = jnp.einsum('ijab,abe->ije', outer, weight_out, precision=lax.Precision.HIGHEST) + final_offset
        return result.astype(jnp.bfloat16)
    return lax.map(one_block, blocks).reshape(AMINO_TOTAL, AMINO_TOTAL, OUTC)
```

```python
import jax
import jax.numpy as jnp
from jax import lax
from jax.experimental import pallas as pl
from jax.experimental.pallas import tpu as pltpu
from jax.sharding import PartitionSpec as P

MESH = pl.DeviceIdType.MESH
BF16, F32 = jnp.bfloat16, jnp.float32
SEQ, RES, CH = 32, 128, 256
HALF, OUTC = 32, 128
ROWS, COLS = 16, 8
SEQ_ALL = SEQ * ROWS
OCT = 8
PIECE = OCT * HALF
NQ = 4
QL = HALF * RES // NQ
NT = (((1,), (1,)), ((), ()))

R_ROLES = ("sib", "xp", "dn", "up", "oa", "ob", "xdn", "xup", "xoa", "xob")
L_ROLES = ("xp", "dn", "up", "oa", "ob", "xdn", "xup", "xoa", "xob")


def project(x_ref, scale_ref, wl_ref, wr_ref, z_ref):
    wt = jnp.concatenate([wl_ref[...], wr_ref[...]], axis=1).astype(F32).T * scale_ref[...]
    hi = wt.astype(BF16)
    lo = (wt - hi.astype(F32)).astype(BF16)
    colsum = jnp.sum(hi.astype(F32) + lo.astype(F32), axis=1, keepdims=True)
    ones = jnp.ones((16, CH), BF16)
    lhs = jnp.concatenate([hi, lo, ones], axis=0)
    step = 8

    def chunk(k, carry):
        xc = x_ref[pl.ds(k * step, step)].reshape(step * RES, CH)
        p = lax.dot_general(lhs, xc, NT, preferred_element_type=F32)
        xf = xc.astype(F32)
        sq = xf * xf
        sqh = sq.astype(BF16)
        sql = (sq - sqh.astype(F32)).astype(BF16)
        s2 = lax.dot_general(ones, sqh, NT, preferred_element_type=F32) + lax.dot_general(
            ones, sql, NT, preferred_element_type=F32
        )
        mean = p[128:136] * (1.0 / CH)
        mh = mean.astype(BF16).astype(F32)
        ml = mean - mh
        var = (s2[0:8] * (1.0 / CH) - mh * mh) - ml * (2.0 * mh + ml)
        rstd = lax.rsqrt(jnp.maximum(var, 0.0) + 1e-05)
        y = (p[0:64] + p[64:128] - colsum * mean[0:1]) * rstd[0:1]
        for s in range(step):
            z_ref[k * step + s] = y[:, s * RES : (s + 1) * RES]
        return carry

    lax.fori_loop(0, SEQ // step, chunk, 0)


def kernel(
    x_ref, scale_ref, wl_ref, wr_ref, w_ref, off_ref, out_ref,
    z_ref, zl_ref, yl_ref, lsend, lt, lf, rf, w2t, wf, outv,
    t_ss, t_rs, l_ss, l_rs, r_ss, r_rs, f_ss, f_rs, o_s,
):
    r, c = lax.axis_index("row"), lax.axis_index("col")
    xl, z, h = r // 8, (r // 2) % 4, r % 2
    xh, y = c // 4, c % 4

    def row_of(xl_, z_, h_):
        return xl_ * 8 + lax.rem(z_ + 4, 4) * 2 + h_

    def col_of(xh_, y_):
        return xh_ * 4 + lax.rem(y_ + 4, 4)

    sib = (row_of(xl, z, 1 - h), c)
    r_dev = {"xp": (row_of(1 - xl, z, h), c), "up": (row_of(xl, z + 1, h), c), "dn": (row_of(xl, z - 1, h), c)}
    l_dev = {"xp": (r, col_of(1 - xh, y)), "up": (r, col_of(xh, y + 1)), "dn": (r, col_of(xh, y - 1))}

    barrier = pltpu.get_barrier_semaphore()
    owner = r // 2
    for dev in (sib, *r_dev.values(), *l_dev.values()):
        pl.semaphore_signal(barrier, inc=1, device_id=dev, device_id_type=MESH)
    for k in range(ROWS):

        @pl.when(jnp.logical_or(k != r, owner != c))
        def _():
            pl.semaphore_signal(barrier, inc=1, device_id=(k, owner), device_id_type=MESH)

    project(x_ref, scale_ref, wl_ref, wr_ref, z_ref)

    for a in range(HALF):
        yl_ref[a] = z_ref[:, a, :].astype(BF16)
    eye = (
        lax.broadcasted_iota(jnp.int32, (RES, RES), 0) == lax.broadcasted_iota(jnp.int32, (RES, RES), 1)
    ).astype(BF16)
    for t in range(8):
        b = jnp.concatenate([yl_ref[t + 8 * g] for g in range(4)], axis=0)
        zl_ref[:, t, :] = lax.dot_general(eye, b, NT, preferred_element_type=F32)
    lsend[...] = zl_ref[...].reshape(RES * 8, 128).astype(BF16)

    pl.semaphore_wait(barrier, jnp.where(owner == c, 22, 23))

    for k in range(ROWS):
        o = lax.rem(r + k, ROWS)
        to_row, to_col = 2 * c + o // COLS, lax.rem(o, COLS)
        src = lsend.at[pl.ds(pl.multiple_of(o * 64, 64), 64)]
        mine = jnp.logical_and(to_row == r, to_col == c)

        @pl.when(mine)
        def _():
            pltpu.make_async_copy(src, lt.at[r], t_rs.at[r]).start()

        @pl.when(jnp.logical_not(mine))
        def _():
            pltpu.make_async_remote_copy(
                src, lt.at[r], t_ss.at[k], t_rs.at[r], device_id=(to_row, to_col), device_id_type=MESH
            ).start()

    for b in range(HALF):
        rf[pl.ds(pl.multiple_of(r * SEQ, SEQ), SEQ), pl.ds(b * RES, RES)] = z_ref[:, HALF + b, :].astype(BF16)

    def r_ref(q, xl_, z_, h_, half=None):
        rows = row_of(xl_, z_, h_) * SEQ
        n = SEQ
        if half is not None:
            rows, n = rows + half * (SEQ // 2), SEQ // 2
        return rf.at[pl.ds(pl.multiple_of(rows, n), n), pl.ds(q * QL, QL)]

    def r_block(q, role, h_):
        return {
            "own": lambda: r_ref(q, xl, z, h_),
            "xp": lambda: r_ref(q, 1 - xl, z, h_),
            "dn": lambda: r_ref(q, xl, z - 1, h_),
            "up": lambda: r_ref(q, xl, z + 1, h_),
            "oa": lambda: r_ref(q, xl, z + 2, h_, 0),
            "ob": lambda: r_ref(q, xl, z + 2, h_, 1),
            "xdn": lambda: r_ref(q, 1 - xl, z - 1, h_),
            "xup": lambda: r_ref(q, 1 - xl, z + 1, h_),
            "xoa": lambda: r_ref(q, 1 - xl, z + 2, h_, 0),
            "xob": lambda: r_ref(q, 1 - xl, z + 2, h_, 1),
        }[role]()

    def copy(src, sems, at, dev):
        return pltpu.make_async_remote_copy(
            src, src, sems[0].at[at], sems[1].at[at], device_id=dev, device_id_type=MESH
        )

    sends = []

    def r_send(q, role, src, dev):
        d = copy(src, (r_ss, r_rs), (q, R_ROLES.index(role)), dev)
        d.start()
        sends.append(d)

    def f_send(q, role):
        d = copy(r_block(q, role, h), (f_ss, f_rs), (q, R_ROLES.index(role)), sib)
        d.start()
        sends.append(d)

    def r_wait(q, role):
        ref = r_block(q, "own" if role == "sib" else role, 1 - h if role == "sib" else h)
        pltpu.make_async_copy(ref, ref, r_rs.at[q, R_ROLES.index(role)]).wait()

    def f_wait(q, role):
        ref = r_block(q, role, 1 - h)
        pltpu.make_async_copy(ref, ref, f_rs.at[q, R_ROLES.index(role)]).wait()

    def r_stage0(q):
        own = r_ref(q, xl, z, h)
        r_send(q, "xp", own, r_dev["xp"])
        r_send(q, "dn", own, r_dev["up"])
        r_send(q, "up", own, r_dev["dn"])
        r_send(q, "sib", own, sib)

    def r_stage1(q):
        r_wait(q, "dn")
        r_send(q, "oa", r_ref(q, xl, z - 1, h, 0), r_dev["up"])
        r_wait(q, "up")
        r_send(q, "ob", r_ref(q, xl, z + 1, h, 1), r_dev["dn"])
        r_wait(q, "xp")
        xp = r_block(q, "xp", h)
        r_send(q, "xdn", xp, r_dev["up"])
        r_send(q, "xup", xp, r_dev["dn"])
        for role in ("dn", "up", "xp"):
            f_send(q, role)

    def r_stage2(q):
        r_wait(q, "xdn")
        r_send(q, "xoa", r_ref(q, 1 - xl, z - 1, h, 0), r_dev["up"])
        r_wait(q, "xup")
        r_send(q, "xob", r_ref(q, 1 - xl, z + 1, h, 1), r_dev["dn"])
        for role in ("xdn", "xup"):
            f_send(q, role)
        for role in ("oa", "ob"):
            r_wait(q, role)
            f_send(q, role)

    def r_stage3(q):
        for role in ("xoa", "xob"):
            r_wait(q, role)
            f_send(q, role)

    def r_stage4(q):
        r_wait(q, "sib")
        for role in R_ROLES[1:]:
            f_wait(q, role)

    def l_ref(xh_, y_, half=None):
        rows, n = col_of(xh_, y_) * PIECE, PIECE
        if half is not None:
            rows, n = rows + half * (PIECE // 2), PIECE // 2
        return lf.at[pl.ds(pl.multiple_of(rows, n), n)]

    def l_block(role):
        return {
            "xp": lambda: l_ref(1 - xh, y),
            "dn": lambda: l_ref(xh, y - 1),
            "up": lambda: l_ref(xh, y + 1),
            "oa": lambda: l_ref(xh, y + 2, 0),
            "ob": lambda: l_ref(xh, y + 2, 1),
            "xdn": lambda: l_ref(1 - xh, y - 1),
            "xup": lambda: l_ref(1 - xh, y + 1),
            "xoa": lambda: l_ref(1 - xh, y + 2, 0),
            "xob": lambda: l_ref(1 - xh, y + 2, 1),
        }[role]()

    def l_send(role, src, dev):
        d = copy(src, (l_ss, l_rs), (L_ROLES.index(role),), dev)
        d.start()
        sends.append(d)

    def l_wait(role):
        ref = l_block(role)
        pltpu.make_async_copy(ref, ref, l_rs.at[L_ROLES.index(role)]).wait()

    def l_stage0():
        for k in range(ROWS):
            pltpu.make_async_copy(lt.at[k], lt.at[k], t_rs.at[k]).wait()
        i0 = lax.broadcasted_iota(jnp.int32, (512, 512), 0)
        i1 = lax.broadcasted_iota(jnp.int32, (512, 512), 1)
        to = ((i0 // 32) % 4) * 128 + (i0 // 128) * 32 + i0 % 32
        perm = (to == i1).astype(BF16)
        for g in range(4):
            v = jnp.concatenate([lt[4 * g + k] for k in range(4)], axis=1)
            w = jnp.dot(v, perm, preferred_element_type=F32)
            w = jnp.concatenate([w[:, 128 * k : 128 * (k + 1)].reshape(OCT, 8, 128) for k in range(4)], axis=1)
            lf[pl.ds(pl.multiple_of(c * PIECE, PIECE), PIECE), pl.ds(g * 128, 128)] = w.reshape(PIECE, 128).astype(BF16)
        own = l_ref(xh, y)
        l_send("xp", own, l_dev["xp"])
        l_send("dn", own, l_dev["up"])
        l_send("up", own, l_dev["dn"])

    def l_stage1():
        l_wait("dn")
        l_send("oa", l_ref(xh, y - 1, 0), l_dev["up"])
        l_wait("up")
        l_send("ob", l_ref(xh, y + 1, 1), l_dev["dn"])
        l_wait("xp")
        xp = l_ref(1 - xh, y)
        l_send("xdn", xp, l_dev["up"])
        l_send("xup", xp, l_dev["dn"])

    def l_stage2():
        l_wait("xdn")
        l_send("xoa", l_ref(1 - xh, y - 1, 0), l_dev["up"])
        l_wait("xup")
        l_send("xob", l_ref(1 - xh, y + 1, 1), l_dev["dn"])

    def l_stage3():
        for role in ("oa", "ob", "xoa", "xob"):
            l_wait(role)

    for q in range(NQ):
        r_stage0(q)
    l_stage0()

    wf[...] = w_ref[...].astype(F32).reshape(HALF, HALF, OUTC)
    for b in range(HALF):
        w2t[:, pl.ds(b * HALF, HALF)] = wf[:, b, :].T.astype(BF16)

    r_stage1(0)
    r_stage1(1)
    l_stage1()
    r_stage2(0)
    r_stage1(2)
    r_stage2(1)
    r_stage3(0)
    r_stage1(3)
    r_stage2(2)
    r_stage3(1)
    l_stage2()
    r_stage2(3)
    r_stage3(2)
    r_stage3(3)
    for q in range(NQ):
        r_stage4(q)
    l_stage3()

    off = off_ref[...]

    def piece(m, carry):
        lhs = lf[pl.ds(pl.multiple_of(m * PIECE, PIECE), PIECE)]
        acc = jnp.zeros((OUTC, OCT * RES), F32)
        for q in range(NQ):
            o = jnp.dot(lhs, rf[:, q * QL : (q + 1) * QL], preferred_element_type=F32).astype(BF16)
            rhs = jnp.concatenate(
                [
                    jnp.concatenate([o[i * HALF : (i + 1) * HALF, b * RES : (b + 1) * RES] for b in range(8)], axis=0)
                    for i in range(OCT)
                ],
                axis=1,
            )
            acc += jnp.dot(w2t[:, q * 256 : (q + 1) * 256], rhs, preferred_element_type=F32)
        for i in range(OCT):
            t = acc[:, i * RES : (i + 1) * RES].T
            outv[m * OCT + i] = (t * (1.0 / SEQ_ALL) + off).astype(BF16)
        rows = pl.ds(m * OCT, OCT)
        pltpu.make_async_copy(outv.at[rows], out_ref.at[rows], o_s.at[m]).start()
        return carry

    lax.fori_loop(0, COLS, piece, 0)
    for m in range(COLS):
        rows = pl.ds(m * OCT, OCT)
        pltpu.make_async_copy(outv.at[rows], out_ref.at[rows], o_s.at[m]).wait()
    for k in range(ROWS):
        o = lax.rem(r + k, ROWS)
        mine = jnp.logical_and(2 * c + o // COLS == r, lax.rem(o, COLS) == c)

        @pl.when(jnp.logical_not(mine))
        def _():
            src = lsend.at[pl.ds(pl.multiple_of(o * 64, 64), 64)]
            pltpu.make_async_copy(src, src, t_ss.at[k]).wait()

    for d in sends:
        d.wait_send()


def body(x, scale, wl, wr, w, off):
    dma = pltpu.SemaphoreType.DMA
    vmem = pl.BlockSpec(memory_space=pltpu.VMEM)
    return pl.pallas_call(
        kernel,
        out_shape=jax.ShapeDtypeStruct((64, RES, OUTC), BF16),
        in_specs=[vmem] * 6,
        out_specs=pl.BlockSpec(memory_space=pl.ANY),
        scratch_shapes=[
            pltpu.VMEM((SEQ, 64, RES), F32),
            pltpu.VMEM((RES, 8, 128), F32),
            pltpu.VMEM((HALF, SEQ, RES), BF16),
            pltpu.VMEM((RES * 8, 128), BF16),
            pltpu.VMEM((ROWS, 64, 128), BF16),
            pltpu.VMEM((COLS * PIECE, SEQ_ALL), BF16),
            pltpu.VMEM((SEQ_ALL, HALF * RES), BF16),
            pltpu.VMEM((OUTC, HALF * HALF), BF16),
            pltpu.VMEM((HALF, HALF, OUTC), F32),
            pltpu.VMEM((64, RES, OUTC), BF16),
            dma((ROWS,)), dma((ROWS,)),
            dma((len(L_ROLES),)), dma((len(L_ROLES),)),
            dma((NQ, len(R_ROLES))), dma((NQ, len(R_ROLES))),
            dma((NQ, len(R_ROLES))), dma((NQ, len(R_ROLES))),
            dma((COLS,)),
        ],
        compiler_params=pltpu.CompilerParams(
            collective_id=0, has_side_effects=True, vmem_limit_bytes=48 * 2**20
        ),
        cost_estimate=pl.CostEstimate(flops=11 * 10**9, bytes_accessed=5 * 10**6, transcendentals=4096),
        name="outer_product_mean",
    )(x, scale.reshape(1, CH), wl, wr, w, off.reshape(1, OUTC))


def solution(mesh):
    in_specs = (P("row", "col", None), P(), P(), P(), P(), P())
    return jax.shard_map(body, mesh=mesh, in_specs=in_specs, out_specs=P("row", "col", None), check_vma=False)
```

```python
import jax
import jax.numpy as jnp
from jax import lax
from jax.experimental import pallas as pl
from jax.experimental.pallas import tpu as pltpu
from jax.sharding import PartitionSpec as P

MESH = pl.DeviceIdType.MESH
BF16, F32 = jnp.bfloat16, jnp.float32
SEQ, RES, CH = 32, 128, 256
HALF, OUTC = 32, 128
ROWS, COLS = 16, 8
SEQ_ALL = SEQ * ROWS
OCT = 8
PIECE = OCT * HALF
NQ = 2
NC = 2
QL = HALF * RES // NQ
QC = HALF * RES // NC
SSTEP = 8
NT = (((1,), (1,)), ((), ()))

R_ROLES = ("sib", "xp", "dn", "up", "oa", "ob", "xdn", "xup", "xoa", "xob")
L_ROLES = ("xp", "dn", "up", "xdn", "xup", "o", "xo")
SUB = 4
EARLY = 2
TRIGGER, TRIGGER_FROM = 'xup', 0
PARTS = (0, 1)
Z_FIRST = (1,)

ORDER = (
    ('e', (
        "r sib 0", "r sib 1", "r xp 0", "r dn 0", "r up 0", "f xp 0", "T", "f dn 0", "f up 0", "r xp 1",
        "f xp 1", "r dn 1", "r up 1", "f dn 1", "f up 1", "l dn 0", "l up 2", "r xdn 0", "r xup 0", "l dn 1",
        "l up 3", "l xp 0", "f xdn 0", "f xup 0", "r oa 0", "r ob 0", "l dn 2", "l up 0", "l xp 2", "f oa 0",
        "f ob 0", "r oa 1", "r ob 1", "l dn 3", "l up 1", "l xp 1", "f oa 1", "f ob 1", "r xoa 0", "r xob 0",
        "l o 0", "l o 2", "l xp 3", "r xdn 1", "f xoa 0", "f xob 0",
    )),
    ('c', (
        (0, 1, 0),
    )),
    ('e', (
        "l o 1", "l o 3", "f xdn 1",
    )),
    ('c', (
        (1, 2, 0),
    )),
    ('e', (
        "l xdn 0", "l xup 0",
    )),
    ('c', (
        (2, 3, 0),
    )),
    ('e', (
        "r xup 1",
    )),
    ('c', (
        (3, 4, 0),
    )),
    ('e', (
        "l xdn 2", "r xoa 1", "l xup 2", "f xup 1",
    )),
    ('c', (
        (4, 5, 0),
    )),
    ('e', (
        "r xob 1", "l xdn 1", "l xup 1", "f xoa 1", "f xob 1",
    )),
    ('c', (
        (0, 1, 1),
    )),
    ('e', (
        "l xdn 3", "l xup 3",
    )),
    ('c', (
        (5, 6, 0),
    )),
    ('e', (
        "l xo 0", "l xo 2",
    )),
    ('c', (
        (6, 7, 0),
    )),
    ('e', (
        "l xo 1",
    )),
    ('c', (
        (1, 3, 1),
    )),
    ('e', (
        "l xo 3",
    )),
    ('c', (
        (7, 8, 0), (3, 8, 1),
    )),
)


def project(x_hbm, x_ref, x_s, scale_ref, wl_ref, wr_ref, z_ref):
    wt = jnp.concatenate([wl_ref[...], wr_ref[...]], axis=0).astype(F32) * scale_ref[...]
    hi = wt.astype(BF16)
    lo = (wt - hi.astype(F32)).astype(BF16)
    colsum = jnp.sum(hi.astype(F32) + lo.astype(F32), axis=1, keepdims=True)
    ones = jnp.ones((16, CH), BF16)
    lhs = jnp.concatenate([hi, lo, ones], axis=0)

    def chunk(k, carry):
        rows = pl.ds(k * SSTEP, SSTEP)
        pltpu.make_async_copy(x_hbm.at[rows], x_ref.at[rows], x_s.at[k]).wait()
        xc = x_ref[rows].reshape(SSTEP * RES, CH)
        p = lax.dot_general(lhs, xc, NT, preferred_element_type=F32)
        xf = xc.astype(F32)
        sq = xf * xf
        sqh = sq.astype(BF16)
        sql = (sq - sqh.astype(F32)).astype(BF16)
        s2 = lax.dot_general(ones, sqh, NT, preferred_element_type=F32) + lax.dot_general(
            ones, sql, NT, preferred_element_type=F32
        )
        mean = p[128:136] * (1.0 / CH)
        mh = mean.astype(BF16).astype(F32)
        ml = mean - mh
        var = (s2[0:8] * (1.0 / CH) - mh * mh) - ml * (2.0 * mh + ml)
        rstd = lax.rsqrt(jnp.maximum(var, 0.0) + 1e-05)
        y = (p[0:64] + p[64:128] - colsum * mean[0:1]) * rstd[0:1]
        for s in range(SSTEP):
            z_ref[k * SSTEP + s] = y[:, s * RES : (s + 1) * RES]
        return carry

    lax.fori_loop(0, SEQ // SSTEP, chunk, 0)


def kernel(
    x_hbm, scale_hbm, wl_hbm, wr_hbm, w_hbm, off_hbm, out_ref,
    x_ref, scale_ref, wl_ref, wr_ref, w_ref, off_ref,
    z_ref, zl_ref, yl_ref, lsend, lt, lf, rf, w2t, wf, ob, acc, outv,
    x_s, p_s, o_s, t_ss, t_rs, l_ss, l_rs, r_ss, r_rs, f_ss, f_rs,
):
    params = ((scale_hbm, scale_ref), (wl_hbm, wl_ref), (wr_hbm, wr_ref), (w_hbm, w_ref), (off_hbm, off_ref))
    params = [pltpu.make_async_copy(a, b, p_s.at[k]) for k, (a, b) in enumerate(params)]
    for d in params[:3]:
        d.start()
    for k in range(SEQ // SSTEP):
        rows = pl.ds(k * SSTEP, SSTEP)
        pltpu.make_async_copy(x_hbm.at[rows], x_ref.at[rows], x_s.at[k]).start()
    for d in params[3:]:
        d.start()

    r, c = lax.axis_index("row"), lax.axis_index("col")
    xl, z, h = r // 8, (r // 2) % 4, r % 2
    xh, y = c // 4, c % 4

    def row_of(xl_, z_, h_):
        return xl_ * 8 + lax.rem(z_ + 4, 4) * 2 + h_

    def col_of(xh_, y_):
        return xh_ * 4 + lax.rem(y_ + 4, 4)

    sib = (row_of(xl, z, 1 - h), c)
    r_dev = {"xp": (row_of(1 - xl, z, h), c), "up": (row_of(xl, z + 1, h), c), "dn": (row_of(xl, z - 1, h), c)}
    l_dev = {"xp": (r, col_of(1 - xh, y)), "up": (r, col_of(xh, y + 1)), "dn": (r, col_of(xh, y - 1))}

    barrier = pltpu.get_barrier_semaphore()
    owner = r // 2
    for dev in (sib, *r_dev.values(), *l_dev.values()):
        pl.semaphore_signal(barrier, inc=1, device_id=dev, device_id_type=MESH)
    for k in range(ROWS):

        @pl.when(jnp.logical_or(k != r, owner != c))
        def _():
            pl.semaphore_signal(barrier, inc=1, device_id=(k, owner), device_id_type=MESH)

    for d in params[:3]:
        d.wait()
    project(x_hbm, x_ref, x_s, scale_ref, wl_ref, wr_ref, z_ref)

    for a in range(HALF):
        yl_ref[a] = z_ref[:, a, :].astype(BF16)
    eye = (
        lax.broadcasted_iota(jnp.int32, (RES, RES), 0) == lax.broadcasted_iota(jnp.int32, (RES, RES), 1)
    ).astype(BF16)
    for t in range(8):
        b = jnp.concatenate([yl_ref[t + 8 * g] for g in range(4)], axis=0)
        zl_ref[:, t, :] = lax.dot_general(eye, b, NT, preferred_element_type=F32)
    lsend[...] = zl_ref[...].reshape(RES * 8, 128).astype(BF16)

    pl.semaphore_wait(barrier, jnp.where(owner == c, 22, 23))

    for k in range(ROWS):
        o = lax.rem(r + k, ROWS)
        to_row, to_col = 2 * c + o // COLS, lax.rem(o, COLS)
        src = lsend.at[pl.ds(pl.multiple_of(o * 64, 64), 64)]
        mine = jnp.logical_and(to_row == r, to_col == c)

        @pl.when(mine)
        def _():
            pltpu.make_async_copy(src, lt.at[r], t_rs.at[r]).start()

        @pl.when(jnp.logical_not(mine))
        def _():
            pltpu.make_async_remote_copy(
                src, lt.at[r], t_ss.at[k], t_rs.at[r], device_id=(to_row, to_col), device_id_type=MESH
            ).start()

    for b in range(HALF):
        rf[pl.ds(pl.multiple_of(r * SEQ, SEQ), SEQ), pl.ds(b * RES, RES)] = z_ref[:, HALF + b, :].astype(BF16)

    def r_ref(q, xl_, z_, h_, half=None):
        rows = row_of(xl_, z_, h_) * SEQ
        n = SEQ
        if half is not None:
            rows, n = rows + half * (SEQ // 2), SEQ // 2
        return rf.at[pl.ds(pl.multiple_of(rows, n), n), pl.ds(q * QL, QL)]

    def r_block(q, role, h_):
        return {
            "own": lambda: r_ref(q, xl, z, h_),
            "xp": lambda: r_ref(q, 1 - xl, z, h_),
            "dn": lambda: r_ref(q, xl, z - 1, h_),
            "up": lambda: r_ref(q, xl, z + 1, h_),
            "oa": lambda: r_ref(q, xl, z + 2, h_, 0),
            "ob": lambda: r_ref(q, xl, z + 2, h_, 1),
            "xdn": lambda: r_ref(q, 1 - xl, z - 1, h_),
            "xup": lambda: r_ref(q, 1 - xl, z + 1, h_),
            "xoa": lambda: r_ref(q, 1 - xl, z + 2, h_, 0),
            "xob": lambda: r_ref(q, 1 - xl, z + 2, h_, 1),
        }[role]()

    def copy(src, sems, at, dev):
        return pltpu.make_async_remote_copy(
            src, src, sems[0].at[at], sems[1].at[at], device_id=dev, device_id_type=MESH
        )

    sends = []

    def r_send(q, role, src, dev):
        d = copy(src, (r_ss, r_rs), (q, R_ROLES.index(role)), dev)
        d.start()
        sends.append(d)

    def f_send(q, role):
        d = copy(r_block(q, role, h), (f_ss, f_rs), (q, R_ROLES.index(role)), sib)
        d.start()
        sends.append(d)

    def r_wait(q, role):
        ref = r_block(q, "own" if role == "sib" else role, 1 - h if role == "sib" else h)
        pltpu.make_async_copy(ref, ref, r_rs.at[q, R_ROLES.index(role)]).wait()

    def f_wait(q, role):
        ref = r_block(q, role, 1 - h)
        pltpu.make_async_copy(ref, ref, f_rs.at[q, R_ROLES.index(role)]).wait()

    def r_own(q):
        own = r_ref(q, xl, z, h)
        r_send(q, "dn", own, r_dev["up"])
        r_send(q, "up", own, r_dev["dn"])
        r_send(q, "xp", own, r_dev["xp"])
        r_send(q, "sib", own, sib)

    def r_event(role, q):
        r_wait(q, role)
        crossed = q not in Z_FIRST
        if role == "dn":
            r_send(q, "oa", r_ref(q, xl, z - 1, h, 0), r_dev["up"])
        elif role == "up":
            r_send(q, "ob", r_ref(q, xl, z + 1, h, 1), r_dev["dn"])
        elif role == "xp" and crossed:
            r_send(q, "xdn", r_block(q, "xp", h), r_dev["up"])
            r_send(q, "xup", r_block(q, "xp", h), r_dev["dn"])
        elif role == "xdn" and crossed:
            r_send(q, "xoa", r_ref(q, 1 - xl, z - 1, h, 0), r_dev["up"])
        elif role == "xup" and crossed:
            r_send(q, "xob", r_ref(q, 1 - xl, z + 1, h, 1), r_dev["dn"])
        if not crossed and role in ("dn", "up", "oa", "ob"):
            r_send(q, "x" + role, r_block(q, role, h), r_dev["xp"])
        if role == TRIGGER and later and q >= TRIGGER_FROM:
            r_own(later.pop(0))
        if role != "sib":
            f_send(q, role)

    l_at = {
        "own": (xh, y), "xp": (1 - xh, y), "dn": (xh, y - 1), "up": (xh, y + 1),
        "xdn": (1 - xh, y - 1), "xup": (1 - xh, y + 1), "o": (xh, y + 2), "xo": (1 - xh, y + 2),
    }
    asc = list(range(SUB))
    desc = asc[SUB // 2 :] + asc[: SUB // 2]

    def l_ref(role, k):
        n = PIECE // SUB
        return lf.at[pl.ds(pl.multiple_of(col_of(*l_at[role]) * PIECE + k * n, n), n)]

    def l_send(role, k, src, dev):
        d = copy(l_ref(src, k), (l_ss, l_rs), (L_ROLES.index(role), k), l_dev[dev])
        d.start()
        sends.append(d)

    def l_wait(role, k):
        ref = l_ref(role, k)
        pltpu.make_async_copy(ref, ref, l_rs.at[L_ROLES.index(role), k]).wait()

    def l_own():
        for k in range(ROWS):
            pltpu.make_async_copy(lt.at[k], lt.at[k], t_rs.at[k]).wait()
        for g in range(4):
            v = jnp.concatenate([lt[4 * g + k] for k in range(4)], axis=1)
            w = jnp.dot(v, perm, preferred_element_type=F32)
            w = jnp.concatenate([w[:, 128 * k : 128 * (k + 1)].reshape(OCT, 8, 128) for k in range(4)], axis=1)
            lf[pl.ds(pl.multiple_of(c * PIECE, PIECE), PIECE), pl.ds(g * 128, 128)] = w.reshape(PIECE, 128).astype(BF16)
        for i in range(SUB):
            l_send("dn", asc[i], "own", "up")
            l_send("up", desc[i], "own", "dn")
            k = (asc, desc)[i % 2][i // 2]
            l_send("xp", k, "own", "xp")

    def l_event(role, k):
        l_wait(role, k)
        if role == "dn" and k < SUB // 2:
            l_send("o", k, "dn", "up")
        elif role == "up" and k >= SUB // 2:
            l_send("o", k, "up", "dn")
        elif role == "xp":
            l_send("xdn", k, "xp", "up")
            l_send("xup", k, "xp", "dn")
        elif role == "xdn" and k < SUB // 2:
            l_send("xo", k, "xdn", "up")
        elif role == "xup" and k >= SUB // 2:
            l_send("xo", k, "xup", "dn")

    def event(name):
        if name == "T":
            l_own()
            return
        kind, role, k = name.split()
        {"r": r_event, "l": l_event, "f": lambda role, q: f_wait(q, role)}[kind](role, int(k))


    def piece_of(k):
        flip = jnp.logical_or(k == 3, k >= 5)
        dy = jnp.where(jnp.logical_or(k == 1, k == 5), 3, jnp.where(jnp.logical_or(k == 2, k == 6), 1, 0))
        dy = jnp.where(jnp.logical_or(k == 4, k == 7), 2, dy)
        return col_of(jnp.where(flip, 1 - xh, xh), y + dy)

    nb = QC // RES

    def outer(k, q, slot):
        lhs = lf[pl.ds(pl.multiple_of(piece_of(k) * PIECE, PIECE), PIECE)]
        o = jnp.dot(lhs, rf[:, pl.ds(pl.multiple_of(q * QC, QC), QC)], preferred_element_type=F32).astype(BF16)
        ob[slot] = jnp.concatenate(
            [
                jnp.concatenate([o[i * HALF : (i + 1) * HALF, b * RES : (b + 1) * RES] for b in range(nb)], axis=0)
                for i in range(OCT)
            ],
            axis=1,
        )

    def final(k, q, slot):
        w = w2t[:, pl.ds(pl.multiple_of(q * nb * HALF, nb * HALF), nb * HALF)]
        acc[k] += jnp.dot(w, ob[slot], preferred_element_type=F32)

    def out_copy(k):
        rows = pl.ds(piece_of(k) * OCT, OCT)
        return pltpu.make_async_copy(outv.at[rows], out_ref.at[rows], o_s.at[k])

    def finish(k):
        m = piece_of(k)
        for i in range(OCT):
            t = acc[k, :, i * RES : (i + 1) * RES].T
            outv[m * OCT + i] = (t * (1.0 / SEQ_ALL) + off).astype(BF16)
        out_copy(k).start()

    def run(first, end, q, before, q_before):
        def step(k, before, done):
            pk, pq, slot = before
            if pk is not None:
                final(pk, pq, slot)
            outer(k, q, 1 - slot)
            if done:
                finish(pk)
            return k, jnp.int32(q), 1 - slot

        before = step(jnp.int32(first), before, q_before == NC - 1)
        if first + 1 < end:
            before = lax.fori_loop(first + 1, end, lambda k, b: step(k, b, q == NC - 1), before)
        return before

    later = list(PARTS[EARLY:])
    for q in PARTS[:EARLY]:
        r_own(q)

    acc[...] = jnp.zeros_like(acc)
    for d in params[3:]:
        d.wait()
    off = off_ref[...]
    i0 = lax.broadcasted_iota(jnp.int32, (512, 512), 0)
    i1 = lax.broadcasted_iota(jnp.int32, (512, 512), 1)
    to = ((i0 // 32) % 4) * 128 + (i0 // 128) * 32 + i0 % 32
    perm = (to == i1).astype(BF16)
    wf[...] = w_ref[...].astype(F32).reshape(HALF, HALF, OUTC)
    for t in range(8):
        blk = jnp.concatenate([wf[:, 4 * t + k, :] for k in range(4)], axis=0)
        w2t[:, pl.ds(t * 128, 128)] = blk.T.astype(BF16)

    before, q_before = (None, jnp.int32(0), jnp.int32(0)), None
    for kind, what in ORDER:
        for x in what:
            if kind == "e":
                event(x)
            else:
                before = run(*x, tuple(jnp.int32(v) if v is not None else v for v in before), q_before)
                q_before = x[2]
    final(*before)
    finish(before[0])
    for k in range(COLS):
        out_copy(k).wait()

    for k in range(ROWS):
        o = lax.rem(r + k, ROWS)
        mine = jnp.logical_and(2 * c + o // COLS == r, lax.rem(o, COLS) == c)

        @pl.when(jnp.logical_not(mine))
        def _():
            src = lsend.at[pl.ds(pl.multiple_of(o * 64, 64), 64)]
            pltpu.make_async_copy(src, src, t_ss.at[k]).wait()

    for d in sends:
        d.wait_send()


def body(x, scale, wl, wr, w, off):
    dma = pltpu.SemaphoreType.DMA
    return pl.pallas_call(
        kernel,
        out_shape=jax.ShapeDtypeStruct((64, RES, OUTC), BF16),
        in_specs=[pl.BlockSpec(memory_space=pltpu.HBM)] * 6,
        out_specs=pl.BlockSpec(memory_space=pltpu.HBM),
        scratch_shapes=[
            pltpu.VMEM((SEQ, RES, CH), BF16),
            pltpu.VMEM((1, CH), F32),
            pltpu.VMEM((HALF, CH), BF16),
            pltpu.VMEM((HALF, CH), BF16),
            pltpu.VMEM((HALF * HALF, OUTC), BF16),
            pltpu.VMEM((1, OUTC), F32),
            pltpu.VMEM((SEQ, 64, RES), F32),
            pltpu.VMEM((RES, 8, 128), F32),
            pltpu.VMEM((HALF, SEQ, RES), BF16),
            pltpu.VMEM((RES * 8, 128), BF16),
            pltpu.VMEM((ROWS, 64, 128), BF16),
            pltpu.VMEM((COLS * PIECE, SEQ_ALL), BF16),
            pltpu.VMEM((SEQ_ALL, HALF * RES), BF16),
            pltpu.VMEM((OUTC, HALF * HALF), BF16),
            pltpu.VMEM((HALF, HALF, OUTC), F32),
            pltpu.VMEM((2, QC // RES * HALF, OCT * RES), BF16),
            pltpu.VMEM((COLS, OUTC, OCT * RES), F32),
            pltpu.VMEM((64, RES, OUTC), BF16),
            dma((SEQ // SSTEP,)), dma((5,)), dma((COLS,)),
            dma((ROWS,)), dma((ROWS,)),
            dma((len(L_ROLES), SUB)), dma((len(L_ROLES), SUB)),
            dma((NQ, len(R_ROLES))), dma((NQ, len(R_ROLES))),
            dma((NQ, len(R_ROLES))), dma((NQ, len(R_ROLES))),
        ],
        compiler_params=pltpu.CompilerParams(
            collective_id=0, has_side_effects=True, vmem_limit_bytes=62 * 2**20
        ),
        cost_estimate=pl.CostEstimate(flops=11 * 10**9, bytes_accessed=5 * 10**6, transcendentals=4096),
        name="outer_product_mean",
    )(x, scale.reshape(1, CH), wl.T, wr.T, w, off.reshape(1, OUTC))


def solution(mesh):
    in_specs = (P("row", "col", None), P(), P(), P(), P(), P())
    return jax.shard_map(body, mesh=mesh, in_specs=in_specs, out_specs=P("row", "col", None), check_vma=False)
```

```python
import jax
import jax.numpy as jnp
from jax import lax
from jax.experimental import pallas as pl
from jax.experimental.pallas import tpu as pltpu
from jax.sharding import PartitionSpec as P

MESH = pl.DeviceIdType.MESH
BF16, F32 = jnp.bfloat16, jnp.float32
SEQ, RES, CH = 32, 128, 256
HALF, OUTC = 32, 128
ROWS, COLS = 16, 8
SEQ_ALL = SEQ * ROWS
OCT = 8
PIECE = OCT * HALF
NQ = 4
NC = 4
QL = HALF * RES // NQ
QC = HALF * RES // NC
SSTEP = 8
NT = (((1,), (1,)), ((), ()))

R_ROLES = ("sib", "xp", "dn", "up", "oa", "ob", "xdn", "xup", "xoa", "xob")
PIECES = ("own", "dn", "up", "xp", "o", "xdn", "xup", "xo")
PAIR = 2
SUB = 2
EARLY = 2
TRIGGER, TRIGGER_FROM = 'dn', 0
PARTS = (0, 1, 2, 3)
Z_FIRST = (3,)

ORDER = (
    ('e', (
        "r sib 0", "r sib 1", "r xp 0", "r dn 0", "r up 0", "r xp 1", "r dn 1", "r up 1", "f xp 0", "T",
        "r sib 2", "f dn 0", "f up 0", "f xp 1", "r xdn 0", "r xup 0", "r xp 2", "r sib 3", "f dn 1", "r oa 0",
        "f up 1", "r up 2", "r xp 3", "f xdn 0", "r dn 2", "r ob 0", "f xup 0", "f xp 2", "f oa 0", "f up 2",
        "r xdn 1", "r xup 1", "f xp 3", "f dn 2", "f ob 0", "r oa 1", "l dn 0", "l up 1", "r up 3", "f xdn 1",
        "r dn 3", "r ob 1", "f xup 1", "f oa 1", "l xp 0", "r xoa 0", "r xob 0", "f up 3", "l dn 1", "l up 0",
        "f dn 3", "f ob 1", "r xdn 2", "r xup 2", "r xup 3", "f xoa 0", "f xob 0",
    )),
    ('c', (
        (0, 1, 0),
    )),
    ('e', (
        "r oa 2", "r ob 2", "l xp 1", "r xoa 1", "r xob 1",
    )),
    ('c', (
        (1, 2, 0),
    )),
    ('e', (
        "r xdn 3", "f xdn 2", "r oa 3", "r ob 3", "l o 0", "l o 1", "f xup 2", "f xup 3", "r xoa 2", "r xob 2",
        "f oa 2", "f ob 2", "f xoa 1", "f xob 1",
    )),
    ('c', (
        (0, 2, 1),
    )),
    ('e', (
        "f xdn 3", "f oa 3", "f ob 3", "f xoa 2", "f xob 2", "l xdn 0", "l xup 0", "r xoa 3",
    )),
    ('c', (
        (0, 1, 2),
    )),
    ('e', (
        "r xob 3",
    )),
    ('c', (
        (1, 2, 2),
    )),
    ('e', (
        "f xoa 3", "l xdn 1", "l xup 1",
    )),
    ('c', (
        (2, 3, 0),
    )),
    ('e', (
        "f xob 3",
    )),
    ('c', (
        (2, 3, 1), (2, 3, 2), (0, 1, 3),
    )),
    ('e', (
        "l xo 0",
    )),
    ('c', (
        (1, 3, 3),
    )),
    ('e', (
        "l xo 1",
    )),
    ('c', (
        (3, 4, 0), (3, 4, 1), (3, 4, 2), (3, 4, 3),
    )),
)


def project(x_hbm, x_ref, x_s, scale_ref, wl_ref, wr_ref, z_ref):
    wt = jnp.concatenate([wl_ref[...], wr_ref[...]], axis=0).astype(F32) * scale_ref[...]
    hi = wt.astype(BF16)
    lo = (wt - hi.astype(F32)).astype(BF16)
    colsum = jnp.sum(hi.astype(F32) + lo.astype(F32), axis=1, keepdims=True)
    ones = jnp.ones((16, CH), BF16)
    lhs = jnp.concatenate([hi, lo, ones], axis=0)

    def chunk(k, carry):
        rows = pl.ds(k * SSTEP, SSTEP)
        pltpu.make_async_copy(x_hbm.at[rows], x_ref.at[rows], x_s.at[k]).wait()
        xc = x_ref[rows].reshape(SSTEP * RES, CH)
        p = lax.dot_general(lhs, xc, NT, preferred_element_type=F32)
        xf = xc.astype(F32)
        sq = xf * xf
        sqh = sq.astype(BF16)
        sql = (sq - sqh.astype(F32)).astype(BF16)
        s2 = lax.dot_general(ones, sqh, NT, preferred_element_type=F32) + lax.dot_general(
            ones, sql, NT, preferred_element_type=F32
        )
        mean = p[128:136] * (1.0 / CH)
        mh = mean.astype(BF16).astype(F32)
        ml = mean - mh
        var = (s2[0:8] * (1.0 / CH) - mh * mh) - ml * (2.0 * mh + ml)
        rstd = lax.rsqrt(jnp.maximum(var, 0.0) + 1e-05)
        y = (p[0:64] + p[64:128] - colsum * mean[0:1]) * rstd[0:1]
        for s in range(SSTEP):
            z_ref[k * SSTEP + s] = y[:, s * RES : (s + 1) * RES]
        return carry

    lax.fori_loop(0, SEQ // SSTEP, chunk, 0)


def kernel(
    x_hbm, scale_hbm, wl_hbm, wr_hbm, w_hbm, off_hbm, out_ref,
    x_ref, scale_ref, wl_ref, wr_ref, w_ref, off_ref,
    z_ref, zl_ref, yl_ref, lsend, lt, lf, rf, w2t, wf, ob, acc, outv,
    x_s, p_s, o_s, t_ss, t_rs, l_ss, l_rs, r_ss, r_rs, f_ss, f_rs,
):
    params = ((scale_hbm, scale_ref), (wl_hbm, wl_ref), (wr_hbm, wr_ref), (w_hbm, w_ref), (off_hbm, off_ref))
    params = [pltpu.make_async_copy(a, b, p_s.at[k]) for k, (a, b) in enumerate(params)]
    for d in params[:3]:
        d.start()
    for k in range(SEQ // SSTEP):
        rows = pl.ds(k * SSTEP, SSTEP)
        pltpu.make_async_copy(x_hbm.at[rows], x_ref.at[rows], x_s.at[k]).start()
    for d in params[3:]:
        d.start()

    r, c = lax.axis_index("row"), lax.axis_index("col")
    xl, z, h = r // 8, (r // 2) % 4, r % 2
    xh, y = c // 4, c % 4

    def row_of(xl_, z_, h_):
        return xl_ * 8 + lax.rem(z_ + 4, 4) * 2 + h_

    def col_of(xh_, y_):
        return xh_ * 4 + lax.rem(y_ + 4, 4)

    sib = (row_of(xl, z, 1 - h), c)
    r_dev = {"xp": (row_of(1 - xl, z, h), c), "up": (row_of(xl, z + 1, h), c), "dn": (row_of(xl, z - 1, h), c)}
    l_dev = {"xp": (r, col_of(1 - xh, y)), "up": (r, col_of(xh, y + 1)), "dn": (r, col_of(xh, y - 1))}

    barrier = pltpu.get_barrier_semaphore()
    owner = r // 2
    for dev in (sib, *r_dev.values(), *l_dev.values()):
        pl.semaphore_signal(barrier, inc=1, device_id=dev, device_id_type=MESH)
    for k in range(ROWS):

        @pl.when(jnp.logical_or(k != r, owner != c))
        def _():
            pl.semaphore_signal(barrier, inc=1, device_id=(k, owner), device_id_type=MESH)

    for d in params[:3]:
        d.wait()
    project(x_hbm, x_ref, x_s, scale_ref, wl_ref, wr_ref, z_ref)

    for a in range(HALF):
        yl_ref[a] = z_ref[:, a, :].astype(BF16)
    eye = (
        lax.broadcasted_iota(jnp.int32, (RES, RES), 0) == lax.broadcasted_iota(jnp.int32, (RES, RES), 1)
    ).astype(BF16)
    for t in range(8):
        b = jnp.concatenate([yl_ref[t + 8 * g] for g in range(4)], axis=0)
        zl_ref[:, t, :] = lax.dot_general(eye, b, NT, preferred_element_type=F32)
    lsend[...] = zl_ref[...].reshape(RES * 8, 128).astype(BF16)

    pl.semaphore_wait(barrier, jnp.where(owner == c, 22, 23))

    for k in range(ROWS):
        o = lax.rem(r + k, ROWS)
        to_row, to_col = 2 * c + o // COLS, lax.rem(o, COLS)
        src = lsend.at[pl.ds(pl.multiple_of(o * 64, 64), 64)]
        mine = jnp.logical_and(to_row == r, to_col == c)

        @pl.when(mine)
        def _():
            pltpu.make_async_copy(src, lt.at[r], t_rs.at[r]).start()

        @pl.when(jnp.logical_not(mine))
        def _():
            pltpu.make_async_remote_copy(
                src, lt.at[r], t_ss.at[k], t_rs.at[r], device_id=(to_row, to_col), device_id_type=MESH
            ).start()

    for b in range(HALF):
        rf[pl.ds(pl.multiple_of(r * SEQ, SEQ), SEQ), pl.ds(b * RES, RES)] = z_ref[:, HALF + b, :].astype(BF16)

    def r_ref(q, xl_, z_, h_, half=None):
        rows = row_of(xl_, z_, h_) * SEQ
        n = SEQ
        if half is not None:
            rows, n = rows + half * (SEQ // 2), SEQ // 2
        return rf.at[pl.ds(pl.multiple_of(rows, n), n), pl.ds(q * QL, QL)]

    def r_block(q, role, h_):
        return {
            "own": lambda: r_ref(q, xl, z, h_),
            "xp": lambda: r_ref(q, 1 - xl, z, h_),
            "dn": lambda: r_ref(q, xl, z - 1, h_),
            "up": lambda: r_ref(q, xl, z + 1, h_),
            "oa": lambda: r_ref(q, xl, z + 2, h_, 0),
            "ob": lambda: r_ref(q, xl, z + 2, h_, 1),
            "xdn": lambda: r_ref(q, 1 - xl, z - 1, h_),
            "xup": lambda: r_ref(q, 1 - xl, z + 1, h_),
            "xoa": lambda: r_ref(q, 1 - xl, z + 2, h_, 0),
            "xob": lambda: r_ref(q, 1 - xl, z + 2, h_, 1),
        }[role]()

    def copy(src, sems, at, dev):
        return pltpu.make_async_remote_copy(
            src, src, sems[0].at[at], sems[1].at[at], device_id=dev, device_id_type=MESH
        )

    sends = []

    def r_send(q, role, src, dev):
        d = copy(src, (r_ss, r_rs), (q, R_ROLES.index(role)), dev)
        d.start()
        sends.append(d)

    def f_send(q, role):
        d = copy(r_block(q, role, h), (f_ss, f_rs), (q, R_ROLES.index(role)), sib)
        d.start()
        sends.append(d)

    def r_wait(q, role):
        ref = r_block(q, "own" if role == "sib" else role, 1 - h if role == "sib" else h)
        pltpu.make_async_copy(ref, ref, r_rs.at[q, R_ROLES.index(role)]).wait()

    def f_wait(q, role):
        ref = r_block(q, role, 1 - h)
        pltpu.make_async_copy(ref, ref, f_rs.at[q, R_ROLES.index(role)]).wait()

    def r_own(q):
        own = r_ref(q, xl, z, h)
        r_send(q, "dn", own, r_dev["up"])
        r_send(q, "up", own, r_dev["dn"])
        r_send(q, "xp", own, r_dev["xp"])
        r_send(q, "sib", own, sib)

    def r_event(role, q):
        r_wait(q, role)
        crossed = q not in Z_FIRST
        if role == "dn":
            r_send(q, "oa", r_ref(q, xl, z - 1, h, 0), r_dev["up"])
        elif role == "up":
            r_send(q, "ob", r_ref(q, xl, z + 1, h, 1), r_dev["dn"])
        elif role == "xp" and crossed:
            r_send(q, "xdn", r_block(q, "xp", h), r_dev["up"])
            r_send(q, "xup", r_block(q, "xp", h), r_dev["dn"])
        elif role == "xdn" and crossed:
            r_send(q, "xoa", r_ref(q, 1 - xl, z - 1, h, 0), r_dev["up"])
        elif role == "xup" and crossed:
            r_send(q, "xob", r_ref(q, 1 - xl, z + 1, h, 1), r_dev["dn"])
        if not crossed and role in ("dn", "up", "oa", "ob"):
            r_send(q, "x" + role, r_block(q, role, h), r_dev["xp"])
        if role == TRIGGER and later and q >= TRIGGER_FROM:
            r_own(later.pop(0))
        if role != "sib":
            f_send(q, role)

    asc = list(range(SUB))
    desc = asc[SUB // 2 :] + asc[: SUB // 2]

    def l_ref(role, k):
        n = PIECE // SUB
        return lf.at[pl.ds(PIECES.index(role) * PIECE + k * n, n)]

    def l_send(role, k, src, dev):
        at = (PIECES.index(role), k)
        d = pltpu.make_async_remote_copy(
            l_ref(src, k), l_ref(role, k), l_ss.at[at], l_rs.at[at], device_id=l_dev[dev], device_id_type=MESH
        )
        d.start()
        sends.append(d)

    def l_wait(role, k):
        ref = l_ref(role, k)
        pltpu.make_async_copy(ref, ref, l_rs.at[PIECES.index(role), k]).wait()

    def l_own():
        for k in range(ROWS):
            pltpu.make_async_copy(lt.at[k], lt.at[k], t_rs.at[k]).wait()
        for g in range(4):
            v = jnp.concatenate([lt[4 * g + k] for k in range(4)], axis=1)
            w = jnp.dot(v, perm, preferred_element_type=F32)
            w = jnp.concatenate([w[:, 128 * k : 128 * (k + 1)].reshape(OCT, 8, 128) for k in range(4)], axis=1)
            lf[pl.ds(0, PIECE), pl.ds(g * 128, 128)] = w.reshape(PIECE, 128).astype(BF16)
        for i in range(SUB):
            l_send("dn", asc[i], "own", "up")
            l_send("up", desc[i], "own", "dn")
            k = (asc, desc)[i % 2][i // 2]
            l_send("xp", k, "own", "xp")

    def l_event(role, k):
        l_wait(role, k)
        if role == "dn" and k < SUB // 2:
            l_send("o", k, "dn", "up")
        elif role == "up" and k >= SUB // 2:
            l_send("o", k, "up", "dn")
        elif role == "xp":
            l_send("xdn", k, "xp", "up")
            l_send("xup", k, "xp", "dn")
        elif role == "xdn" and k < SUB // 2:
            l_send("xo", k, "xdn", "up")
        elif role == "xup" and k >= SUB // 2:
            l_send("xo", k, "xup", "dn")

    def event(name):
        if name == "T":
            l_own()
            return
        kind, role, k = name.split()
        {"r": r_event, "l": l_event, "f": lambda role, q: f_wait(q, role)}[kind](role, int(k))


    def piece_of(k):
        flip = jnp.logical_or(k == 3, k >= 5)
        dy = jnp.where(jnp.logical_or(k == 1, k == 5), 3, jnp.where(jnp.logical_or(k == 2, k == 6), 1, 0))
        dy = jnp.where(jnp.logical_or(k == 4, k == 7), 2, dy)
        return col_of(jnp.where(flip, 1 - xh, xh), y + dy)

    nb = QC // RES

    rows = PAIR * OCT

    def outer(p, q, slot):
        lhs = lf[pl.ds(pl.multiple_of(p * PAIR * PIECE, PIECE), PAIR * PIECE)]
        o = jnp.dot(lhs, rf[:, pl.ds(pl.multiple_of(q * QC, QC), QC)], preferred_element_type=F32).astype(BF16)
        ob[slot] = jnp.concatenate(
            [
                jnp.concatenate([o[i * HALF : (i + 1) * HALF, b * RES : (b + 1) * RES] for b in range(nb)], axis=0)
                for i in range(rows)
            ],
            axis=1,
        )

    def final(p, q, slot):
        w = w2t[:, pl.ds(pl.multiple_of(q * nb * HALF, nb * HALF), nb * HALF)]
        acc[p] += jnp.dot(w, ob[slot], preferred_element_type=F32)

    def out_copy(k):
        rows = pl.ds(piece_of(k) * OCT, OCT)
        return pltpu.make_async_copy(outv.at[rows], out_ref.at[rows], o_s.at[k])

    def finish(p):
        for k in range(PAIR):
            m = piece_of(p * PAIR + k)
            for i in range(OCT):
                at = (k * OCT + i) * RES
                t = acc[p, :, at : at + RES].T
                outv[m * OCT + i] = (t * (1.0 / SEQ_ALL) + off).astype(BF16)
            out_copy(p * PAIR + k).start()

    def run(first, end, q, before, q_before):
        def step(k, before, done):
            pk, pq, slot = before
            if pk is not None:
                final(pk, pq, slot)
            outer(k, q, 1 - slot)
            if done:
                finish(pk)
            return k, jnp.int32(q), 1 - slot

        before = step(jnp.int32(first), before, q_before == NC - 1)
        if first + 1 < end:
            before = lax.fori_loop(first + 1, end, lambda k, b: step(k, b, q == NC - 1), before)
        return before

    later = list(PARTS[EARLY:])
    for q in PARTS[:EARLY]:
        r_own(q)

    acc[...] = jnp.zeros_like(acc)
    for d in params[3:]:
        d.wait()
    off = off_ref[...]
    i0 = lax.broadcasted_iota(jnp.int32, (512, 512), 0)
    i1 = lax.broadcasted_iota(jnp.int32, (512, 512), 1)
    to = ((i0 // 32) % 4) * 128 + (i0 // 128) * 32 + i0 % 32
    perm = (to == i1).astype(BF16)
    wf[...] = w_ref[...].astype(F32).reshape(HALF, HALF, OUTC)
    for t in range(8):
        blk = jnp.concatenate([wf[:, 4 * t + k, :] for k in range(4)], axis=0)
        w2t[:, pl.ds(t * 128, 128)] = blk.T.astype(BF16)

    before, q_before = (None, jnp.int32(0), jnp.int32(0)), None
    for kind, what in ORDER:
        for x in what:
            if kind == "e":
                event(x)
            else:
                before = run(*x, tuple(jnp.int32(v) if v is not None else v for v in before), q_before)
                q_before = x[2]
    final(*before)
    finish(before[0])
    for k in range(COLS):
        out_copy(k).wait()

    for k in range(ROWS):
        o = lax.rem(r + k, ROWS)
        mine = jnp.logical_and(2 * c + o // COLS == r, lax.rem(o, COLS) == c)

        @pl.when(jnp.logical_not(mine))
        def _():
            src = lsend.at[pl.ds(pl.multiple_of(o * 64, 64), 64)]
            pltpu.make_async_copy(src, src, t_ss.at[k]).wait()

    for d in sends:
        d.wait_send()


def place(src, dst, held, sems):
    parts = [pl.ds(k * OCT, OCT) for k in range(COLS)]
    ins = [pltpu.make_async_copy(src.at[p], held.at[p], sems.at[0, k]) for k, p in enumerate(parts)]
    outs = [pltpu.make_async_copy(held.at[p], dst.at[p], sems.at[1, k]) for k, p in enumerate(parts)]
    for d in ins:
        d.start()
    for d, e in zip(ins, outs):
        d.wait()
        e.start()
    for e in outs:
        e.wait()


def body(x, scale, wl, wr, w, off):
    dma = pltpu.SemaphoreType.DMA
    out = pl.pallas_call(
        kernel,
        out_shape=jax.ShapeDtypeStruct((64, RES, OUTC), BF16),
        in_specs=[pl.BlockSpec(memory_space=pltpu.HBM)] * 6,
        out_specs=pl.BlockSpec(memory_space=pltpu.HBM),
        scratch_shapes=[
            pltpu.VMEM((SEQ, RES, CH), BF16),
            pltpu.VMEM((1, CH), F32),
            pltpu.VMEM((HALF, CH), BF16),
            pltpu.VMEM((HALF, CH), BF16),
            pltpu.VMEM((HALF * HALF, OUTC), BF16),
            pltpu.VMEM((1, OUTC), F32),
            pltpu.VMEM((SEQ, 64, RES), F32),
            pltpu.VMEM((RES, 8, 128), F32),
            pltpu.VMEM((HALF, SEQ, RES), BF16),
            pltpu.VMEM((RES * 8, 128), BF16),
            pltpu.VMEM((ROWS, 64, 128), BF16),
            pltpu.VMEM((COLS * PIECE, SEQ_ALL), BF16),
            pltpu.VMEM((SEQ_ALL, HALF * RES), BF16),
            pltpu.VMEM((OUTC, HALF * HALF), BF16),
            pltpu.VMEM((HALF, HALF, OUTC), F32),
            pltpu.VMEM((2, QC // RES * HALF, PAIR * OCT * RES), BF16),
            pltpu.VMEM((COLS // PAIR, OUTC, PAIR * OCT * RES), F32),
            pltpu.VMEM((64, RES, OUTC), BF16),
            dma((SEQ // SSTEP,)), dma((5,)), dma((COLS,)),
            dma((ROWS,)), dma((ROWS,)),
            dma((COLS, SUB)), dma((COLS, SUB)),
            dma((NQ, len(R_ROLES))), dma((NQ, len(R_ROLES))),
            dma((NQ, len(R_ROLES))), dma((NQ, len(R_ROLES))),
        ],
        compiler_params=pltpu.CompilerParams(
            collective_id=0, has_side_effects=True, vmem_limit_bytes=62 * 2**20
        ),
        cost_estimate=pl.CostEstimate(flops=11 * 10**9, bytes_accessed=5 * 10**6, transcendentals=4096),
        name="outer_product_mean",
    )(x, scale.reshape(1, CH), wl.T, wr.T, w, off.reshape(1, OUTC))
    return pl.pallas_call(
        place,
        out_shape=jax.ShapeDtypeStruct(out.shape, out.dtype),
        in_specs=[pl.BlockSpec(memory_space=pltpu.HBM)],
        out_specs=pl.BlockSpec(memory_space=pltpu.HBM),
        scratch_shapes=[pltpu.VMEM((64, RES, OUTC), BF16), dma((2, COLS))],
        compiler_params=pltpu.CompilerParams(vmem_limit_bytes=62 * 2**20),
        name="place",
    )(out)


def solution(mesh):
    in_specs = (P("row", "col", None), P(), P(), P(), P(), P())
    return jax.shard_map(body, mesh=mesh, in_specs=in_specs, out_specs=P("row", "col", None), check_vma=False)
```

```python
import jax
import jax.numpy as jnp
from jax import lax
from jax.experimental import pallas as pl
from jax.experimental.pallas import tpu as pltpu
from jax.sharding import PartitionSpec as P

MESH = pl.DeviceIdType.MESH
BF16, F32 = jnp.bfloat16, jnp.float32
SEQ, RES, CH = 32, 128, 256
HALF, OUTC = 32, 128
ROWS, COLS = 16, 8
SEQ_ALL = SEQ * ROWS
OCT = 8
PIECE = OCT * HALF
NQ = 4
NC = 4
QL = HALF * RES // NQ
QC = HALF * RES // NC
SSTEP = 8
NT = (((1,), (1,)), ((), ()))

R_ROLES = ("sib", "xp", "dn", "up", "oa", "ob", "xdn", "xup", "xoa", "xob")
PIECES = ("own", "dn", "up", "xp", "o", "xdn", "xup", "xo")
PAIR = 2
SUB = 2
EARLY = 3
TRIGGER, TRIGGER_FROM = 'dn', 0
PARTS = (0, 1, 2, 3)
Z_FIRST = (3,)

ORDER = (
    ('e', (
        "r sib 0", "r sib 1", "r sib 2", "r xp 0", "r dn 0", "r up 0", "r xp 1", "r dn 1", "r up 1", "f xp 0",
        "T", "r xp 2", "r sib 3", "f dn 0", "f up 0", "f xp 1", "r dn 2", "r up 2", "r xp 3", "f dn 1",
        "f up 1", "r xdn 0", "r xup 0", "f xp 2", "f dn 2", "r oa 0", "f up 2", "f xp 3", "r up 3", "f xdn 0",
        "r dn 3", "r ob 0", "f xup 0", "f oa 0", "l dn 0", "l up 0", "f up 3", "r xdn 1", "r xup 1", "f dn 3",
        "f ob 0", "r oa 1", "r ob 1", "l xp 0", "f xdn 1", "r xdn 2", "r xup 2", "f xup 1", "l dn 1", "l up 1",
        "f oa 1", "f ob 1", "r oa 2", "r ob 2", "r xup 3", "r xoa 0", "r xob 0", "l xp 1", "f xdn 2", "r oa 3",
        "r ob 3", "r xdn 3", "f xup 2", "f oa 2", "f ob 2", "r xoa 1", "r xob 1", "f xup 3", "l o 0",
        "f xoa 0", "f xob 0",
    )),
    ('c', (
        (0, 1, 0),
    )),
    ('e', (
        "r xoa 2", "r xob 2", "l xup 0", "f oa 3", "f ob 3", "f xdn 3",
    )),
    ('c', (
        (1, 2, 0),
    )),
    ('e', (
        "f xoa 1", "r xoa 3", "f xob 1",
    )),
    ('c', (
        (0, 1, 1),
    )),
    ('e', (
        "r xob 3", "l xdn 0", "f xoa 2", "f xob 2",
    )),
    ('c', (
        (1, 2, 1),
    )),
    ('e', (
        "l o 1",
    )),
    ('c', (
        (0, 1, 2),
    )),
    ('e', (
        "f xoa 3",
    )),
    ('c', (
        (1, 2, 2),
    )),
    ('e', (
        "f xob 3", "l xdn 1",
    )),
    ('c', (
        (2, 3, 0),
    )),
    ('e', (
        "l xup 1",
    )),
    ('c', (
        (2, 3, 1),
    )),
    ('e', (
        "l xo 0",
    )),
    ('c', (
        (2, 3, 2), (0, 3, 3),
    )),
    ('e', (
        "l xo 1",
    )),
    ('c', (
        (3, 4, 0), (3, 4, 1), (3, 4, 2), (3, 4, 3),
    )),
)


def project(x_hbm, x_ref, x_s, scale_ref, wl_ref, wr_ref, z_ref):
    wt = jnp.concatenate([wl_ref[...], wr_ref[...]], axis=0).astype(F32) * scale_ref[...]
    hi = wt.astype(BF16)
    lo = (wt - hi.astype(F32)).astype(BF16)
    colsum = jnp.sum(hi.astype(F32) + lo.astype(F32), axis=1, keepdims=True)
    ones = jnp.ones((16, CH), BF16)
    lhs = jnp.concatenate([hi, lo, ones], axis=0)

    def chunk(k, carry):
        rows = pl.ds(k * SSTEP, SSTEP)
        pltpu.make_async_copy(x_hbm.at[rows], x_ref.at[rows], x_s.at[k]).wait()
        xc = x_ref[rows].reshape(SSTEP * RES, CH)
        p = lax.dot_general(lhs, xc, NT, preferred_element_type=F32)
        xf = xc.astype(F32)
        sq = xf * xf
        sqh = sq.astype(BF16)
        sql = (sq - sqh.astype(F32)).astype(BF16)
        s2 = lax.dot_general(ones, sqh, NT, preferred_element_type=F32) + lax.dot_general(
            ones, sql, NT, preferred_element_type=F32
        )
        mean = p[128:136] * (1.0 / CH)
        mh = mean.astype(BF16).astype(F32)
        ml = mean - mh
        var = (s2[0:8] * (1.0 / CH) - mh * mh) - ml * (2.0 * mh + ml)
        rstd = lax.rsqrt(jnp.maximum(var, 0.0) + 1e-05)
        y = (p[0:64] + p[64:128] - colsum * mean[0:1]) * rstd[0:1]
        for s in range(SSTEP):
            z_ref[k * SSTEP + s] = y[:, s * RES : (s + 1) * RES]
        return carry

    lax.fori_loop(0, SEQ // SSTEP, chunk, 0)


def kernel(
    x_hbm, scale_hbm, wl_hbm, wr_hbm, w_hbm, off_hbm, out_ref,
    x_ref, scale_ref, wl_ref, wr_ref, w_ref, off_ref,
    z_ref, zl_ref, yl_ref, lsend, lt, lf, rf, w2t, wf, ob, acc, outv,
    x_s, p_s, o_s, t_ss, t_rs, l_ss, l_rs, r_ss, r_rs, f_ss, f_rs,
):
    params = ((scale_hbm, scale_ref), (wl_hbm, wl_ref), (wr_hbm, wr_ref), (w_hbm, w_ref), (off_hbm, off_ref))
    params = [pltpu.make_async_copy(a, b, p_s.at[k]) for k, (a, b) in enumerate(params)]
    for d in params[:3]:
        d.start()
    for k in range(SEQ // SSTEP):
        rows = pl.ds(k * SSTEP, SSTEP)
        pltpu.make_async_copy(x_hbm.at[rows], x_ref.at[rows], x_s.at[k]).start()
    for d in params[3:]:
        d.start()

    r, c = lax.axis_index("row"), lax.axis_index("col")
    xl, z, h = r // 8, (r // 2) % 4, r % 2
    xh, y = c // 4, c % 4

    def row_of(xl_, z_, h_):
        return xl_ * 8 + lax.rem(z_ + 4, 4) * 2 + h_

    def col_of(xh_, y_):
        return xh_ * 4 + lax.rem(y_ + 4, 4)

    sib = (row_of(xl, z, 1 - h), c)
    r_dev = {"xp": (row_of(1 - xl, z, h), c), "up": (row_of(xl, z + 1, h), c), "dn": (row_of(xl, z - 1, h), c)}
    l_dev = {"xp": (r, col_of(1 - xh, y)), "up": (r, col_of(xh, y + 1)), "dn": (r, col_of(xh, y - 1))}

    barrier = pltpu.get_barrier_semaphore()
    owner = r // 2
    for dev in (sib, *r_dev.values(), *l_dev.values()):
        pl.semaphore_signal(barrier, inc=1, device_id=dev, device_id_type=MESH)
    for k in range(ROWS):

        @pl.when(jnp.logical_or(k != r, owner != c))
        def _():
            pl.semaphore_signal(barrier, inc=1, device_id=(k, owner), device_id_type=MESH)

    for d in params[:3]:
        d.wait()
    project(x_hbm, x_ref, x_s, scale_ref, wl_ref, wr_ref, z_ref)

    for a in range(HALF):
        yl_ref[a] = z_ref[:, a, :].astype(BF16)
    eye = (
        lax.broadcasted_iota(jnp.int32, (RES, RES), 0) == lax.broadcasted_iota(jnp.int32, (RES, RES), 1)
    ).astype(BF16)
    for t in range(8):
        b = jnp.concatenate([yl_ref[t + 8 * g] for g in range(4)], axis=0)
        zl_ref[:, t, :] = lax.dot_general(eye, b, NT, preferred_element_type=F32)
    lsend[...] = zl_ref[...].reshape(RES * 8, 128).astype(BF16)

    pl.semaphore_wait(barrier, jnp.where(owner == c, 22, 23))

    for k in range(ROWS):
        o = k
        to_row, to_col = 2 * c + o // COLS, o % COLS
        src = lsend.at[pl.ds(o * 64, 64)]
        mine = jnp.logical_and(to_row == r, to_col == c)

        @pl.when(mine)
        def _():
            pltpu.make_async_copy(src, lt.at[r], t_rs.at[r]).start()

        @pl.when(jnp.logical_not(mine))
        def _():
            pltpu.make_async_remote_copy(
                src, lt.at[r], t_ss.at[k], t_rs.at[r], device_id=(to_row, to_col), device_id_type=MESH
            ).start()

    for b in range(HALF):
        rf[pl.ds(pl.multiple_of(r * SEQ, SEQ), SEQ), pl.ds(b * RES, RES)] = z_ref[:, HALF + b, :].astype(BF16)

    def r_ref(q, xl_, z_, h_, half=None):
        rows = row_of(xl_, z_, h_) * SEQ
        n = SEQ
        if half is not None:
            rows, n = rows + half * (SEQ // 2), SEQ // 2
        return rf.at[pl.ds(pl.multiple_of(rows, n), n), pl.ds(q * QL, QL)]

    def r_block(q, role, h_):
        return {
            "own": lambda: r_ref(q, xl, z, h_),
            "xp": lambda: r_ref(q, 1 - xl, z, h_),
            "dn": lambda: r_ref(q, xl, z - 1, h_),
            "up": lambda: r_ref(q, xl, z + 1, h_),
            "oa": lambda: r_ref(q, xl, z + 2, h_, 0),
            "ob": lambda: r_ref(q, xl, z + 2, h_, 1),
            "xdn": lambda: r_ref(q, 1 - xl, z - 1, h_),
            "xup": lambda: r_ref(q, 1 - xl, z + 1, h_),
            "xoa": lambda: r_ref(q, 1 - xl, z + 2, h_, 0),
            "xob": lambda: r_ref(q, 1 - xl, z + 2, h_, 1),
        }[role]()

    def copy(src, sems, at, dev):
        return pltpu.make_async_remote_copy(
            src, src, sems[0].at[at], sems[1].at[at], device_id=dev, device_id_type=MESH
        )

    sends = []

    def r_send(q, role, src, dev):
        d = copy(src, (r_ss, r_rs), (q, R_ROLES.index(role)), dev)
        d.start()
        sends.append(d)

    def f_send(q, role):
        d = copy(r_block(q, role, h), (f_ss, f_rs), (q, R_ROLES.index(role)), sib)
        d.start()
        sends.append(d)

    def r_wait(q, role):
        ref = r_block(q, "own" if role == "sib" else role, 1 - h if role == "sib" else h)
        pltpu.make_async_copy(ref, ref, r_rs.at[q, R_ROLES.index(role)]).wait()

    def f_wait(q, role):
        ref = r_block(q, role, 1 - h)
        pltpu.make_async_copy(ref, ref, f_rs.at[q, R_ROLES.index(role)]).wait()

    def r_own(q):
        own = r_ref(q, xl, z, h)
        r_send(q, "xp", own, r_dev["xp"])
        r_send(q, "dn", own, r_dev["up"])
        r_send(q, "up", own, r_dev["dn"])
        r_send(q, "sib", own, sib)

    def r_event(role, q):
        r_wait(q, role)
        crossed = q not in Z_FIRST
        if role == "dn":
            r_send(q, "oa", r_ref(q, xl, z - 1, h, 0), r_dev["up"])
        elif role == "up":
            r_send(q, "ob", r_ref(q, xl, z + 1, h, 1), r_dev["dn"])
        elif role == "xp" and crossed:
            r_send(q, "xdn", r_block(q, "xp", h), r_dev["up"])
            r_send(q, "xup", r_block(q, "xp", h), r_dev["dn"])
        elif role == "xdn" and crossed:
            r_send(q, "xoa", r_ref(q, 1 - xl, z - 1, h, 0), r_dev["up"])
        elif role == "xup" and crossed:
            r_send(q, "xob", r_ref(q, 1 - xl, z + 1, h, 1), r_dev["dn"])
        if not crossed and role in ("dn", "up", "oa", "ob"):
            r_send(q, "x" + role, r_block(q, role, h), r_dev["xp"])
        if role == TRIGGER and later and q >= TRIGGER_FROM:
            r_own(later.pop(0))
        if role != "sib":
            f_send(q, role)

    asc = list(range(SUB))
    desc = asc[SUB // 2 :] + asc[: SUB // 2]

    def l_ref(role, k):
        n = PIECE // SUB
        return lf.at[pl.ds(PIECES.index(role) * PIECE + k * n, n)]

    def l_send(role, k, src, dev):
        at = (PIECES.index(role), k)
        d = pltpu.make_async_remote_copy(
            l_ref(src, k), l_ref(role, k), l_ss.at[at], l_rs.at[at], device_id=l_dev[dev], device_id_type=MESH
        )
        d.start()
        sends.append(d)

    def l_wait(role, k):
        ref = l_ref(role, k)
        pltpu.make_async_copy(ref, ref, l_rs.at[PIECES.index(role), k]).wait()

    def l_own():
        for k in range(ROWS):
            pltpu.make_async_copy(lt.at[k], lt.at[k], t_rs.at[k]).wait()
        v = jnp.concatenate([jnp.concatenate([lt[4 * g + k] for k in range(4)], axis=1) for g in range(4)], axis=0)
        w = jnp.dot(v, perm, preferred_element_type=F32)
        for g in range(4):
            u = [w[64 * g : 64 * (g + 1), 128 * k : 128 * (k + 1)].reshape(OCT, 8, 128) for k in range(4)]
            lf[pl.ds(0, PIECE), pl.ds(g * 128, 128)] = jnp.concatenate(u, axis=1).reshape(PIECE, 128).astype(BF16)
        for i in range(SUB):
            l_send("xp", (asc, desc)[i % 2][i // 2], "own", "xp")
            l_send("dn", asc[i], "own", "up")
            l_send("up", desc[i], "own", "dn")

    def l_event(role, k):
        l_wait(role, k)
        if role == "dn" and k < SUB // 2:
            l_send("o", k, "dn", "up")
        elif role == "up" and k >= SUB // 2:
            l_send("o", k, "up", "dn")
        elif role == "xp":
            l_send("xdn", k, "xp", "up")
            l_send("xup", k, "xp", "dn")
        elif role == "o":
            l_send("xo", k, "o", "xp")

    def event(name):
        if name == "T":
            l_own()
            return
        kind, role, k = name.split()
        {"r": r_event, "l": l_event, "f": lambda role, q: f_wait(q, role)}[kind](role, int(k))


    def piece_of(k):
        flip = jnp.logical_or(k == 3, k >= 5)
        dy = jnp.where(jnp.logical_or(k == 1, k == 5), 3, jnp.where(jnp.logical_or(k == 2, k == 6), 1, 0))
        dy = jnp.where(jnp.logical_or(k == 4, k == 7), 2, dy)
        return col_of(jnp.where(flip, 1 - xh, xh), y + dy)

    nb = QC // RES

    rows = PAIR * OCT

    def outer(p, q, slot):
        lhs = lf[pl.ds(pl.multiple_of(p * PAIR * PIECE, PIECE), PAIR * PIECE)]
        o = jnp.dot(lhs, rf[:, pl.ds(pl.multiple_of(q * QC, QC), QC)], preferred_element_type=F32).astype(BF16)
        ob[slot] = jnp.concatenate(
            [
                jnp.concatenate([o[i * HALF : (i + 1) * HALF, b * RES : (b + 1) * RES] for b in range(nb)], axis=0)
                for i in range(rows)
            ],
            axis=1,
        )

    def final(p, q, slot):
        w = w2t[:, pl.ds(pl.multiple_of(q * nb * HALF, nb * HALF), nb * HALF)]
        acc[p] += jnp.dot(w, ob[slot], preferred_element_type=F32)

    def out_copy(k):
        rows = pl.ds(piece_of(k) * OCT, OCT)
        return pltpu.make_async_copy(outv.at[rows], out_ref.at[rows], o_s.at[k])

    def finish(p):
        for k in range(PAIR):
            m = piece_of(p * PAIR + k)
            for i in range(OCT):
                at = (k * OCT + i) * RES
                t = acc[p, :, at : at + RES].T
                outv[m * OCT + i] = (t * (1.0 / SEQ_ALL) + off).astype(BF16)
            out_copy(p * PAIR + k).start()

    def run(first, end, q, before, q_before):
        def step(k, before, done):
            pk, pq, slot = before
            if pk is not None:
                final(pk, pq, slot)
            outer(k, q, 1 - slot)
            if done:
                finish(pk)
            return k, jnp.int32(q), 1 - slot

        before = step(jnp.int32(first), before, q_before == NC - 1)
        if first + 1 < end:
            before = lax.fori_loop(first + 1, end, lambda k, b: step(k, b, q == NC - 1), before)
        return before

    later = list(PARTS[EARLY:])
    for q in PARTS[:EARLY]:
        r_own(q)

    acc[...] = jnp.zeros_like(acc)
    for d in params[3:]:
        d.wait()
    off = off_ref[...]
    i0 = lax.broadcasted_iota(jnp.int32, (512, 512), 0)
    i1 = lax.broadcasted_iota(jnp.int32, (512, 512), 1)
    to = ((i0 // 32) % 4) * 128 + (i0 // 128) * 32 + i0 % 32
    perm = (to == i1).astype(BF16)
    wf[...] = w_ref[...].astype(F32).reshape(HALF, HALF, OUTC)
    for t in range(8):
        blk = jnp.concatenate([wf[:, 4 * t + k, :] for k in range(4)], axis=0)
        w2t[:, pl.ds(t * 128, 128)] = blk.T.astype(BF16)

    before, q_before = (None, jnp.int32(0), jnp.int32(0)), None
    for kind, what in ORDER:
        for x in what:
            if kind == "e":
                event(x)
            else:
                before = run(*x, tuple(jnp.int32(v) if v is not None else v for v in before), q_before)
                q_before = x[2]
    final(*before)
    finish(before[0])
    for k in range(COLS):
        out_copy(k).wait()

    for k in range(ROWS):
        o = k
        mine = jnp.logical_and(2 * c + o // COLS == r, o % COLS == c)

        @pl.when(jnp.logical_not(mine))
        def _():
            src = lsend.at[pl.ds(o * 64, 64)]
            pltpu.make_async_copy(src, src, t_ss.at[k]).wait()

    for d in sends:
        d.wait_send()


def place(src, dst, held, sems):
    parts = [pl.ds(k * OCT, OCT) for k in range(COLS)]
    ins = [pltpu.make_async_copy(src.at[p], held.at[p], sems.at[0, k]) for k, p in enumerate(parts)]
    outs = [pltpu.make_async_copy(held.at[p], dst.at[p], sems.at[1, k]) for k, p in enumerate(parts)]
    for d in ins:
        d.start()
    for d, e in zip(ins, outs):
        d.wait()
        e.start()
    for e in outs:
        e.wait()


def body(x, scale, wl, wr, w, off):
    dma = pltpu.SemaphoreType.DMA
    out = pl.pallas_call(
        kernel,
        out_shape=jax.ShapeDtypeStruct((64, RES, OUTC), BF16),
        in_specs=[pl.BlockSpec(memory_space=pltpu.HBM)] * 6,
        out_specs=pl.BlockSpec(memory_space=pltpu.HBM),
        scratch_shapes=[
            pltpu.VMEM((SEQ, RES, CH), BF16),
            pltpu.VMEM((1, CH), F32),
            pltpu.VMEM((HALF, CH), BF16),
            pltpu.VMEM((HALF, CH), BF16),
            pltpu.VMEM((HALF * HALF, OUTC), BF16),
            pltpu.VMEM((1, OUTC), F32),
            pltpu.VMEM((SEQ, 64, RES), F32),
            pltpu.VMEM((RES, 8, 128), F32),
            pltpu.VMEM((HALF, SEQ, RES), BF16),
            pltpu.VMEM((RES * 8, 128), BF16),
            pltpu.VMEM((ROWS, 64, 128), BF16),
            pltpu.VMEM((COLS * PIECE, SEQ_ALL), BF16),
            pltpu.VMEM((SEQ_ALL, HALF * RES), BF16),
            pltpu.VMEM((OUTC, HALF * HALF), BF16),
            pltpu.VMEM((HALF, HALF, OUTC), F32),
            pltpu.VMEM((2, QC // RES * HALF, PAIR * OCT * RES), BF16),
            pltpu.VMEM((COLS // PAIR, OUTC, PAIR * OCT * RES), F32),
            pltpu.VMEM((64, RES, OUTC), BF16),
            dma((SEQ // SSTEP,)), dma((5,)), dma((COLS,)),
            dma((ROWS,)), dma((ROWS,)),
            dma((COLS, SUB)), dma((COLS, SUB)),
            dma((NQ, len(R_ROLES))), dma((NQ, len(R_ROLES))),
            dma((NQ, len(R_ROLES))), dma((NQ, len(R_ROLES))),
        ],
        compiler_params=pltpu.CompilerParams(
            collective_id=0, has_side_effects=True, vmem_limit_bytes=62 * 2**20
        ),
        cost_estimate=pl.CostEstimate(flops=11 * 10**9, bytes_accessed=5 * 10**6, transcendentals=4096),
        name="outer_product_mean",
    )(x, scale.reshape(1, CH), wl.T, wr.T, w, off.reshape(1, OUTC))
    return pl.pallas_call(
        place,
        out_shape=jax.ShapeDtypeStruct(out.shape, out.dtype),
        in_specs=[pl.BlockSpec(memory_space=pltpu.HBM)],
        out_specs=pl.BlockSpec(memory_space=pltpu.HBM),
        scratch_shapes=[pltpu.VMEM((64, RES, OUTC), BF16), dma((2, COLS))],
        compiler_params=pltpu.CompilerParams(vmem_limit_bytes=62 * 2**20),
        name="place",
    )(out)


def solution(mesh):
    in_specs = (P("row", "col", None), P(), P(), P(), P(), P())
    return jax.shard_map(body, mesh=mesh, in_specs=in_specs, out_specs=P("row", "col", None), check_vma=False)
```

```python
import jax
import jax.numpy as jnp
from jax import lax
from jax.experimental import pallas as pl
from jax.experimental.pallas import tpu as pltpu
from jax.sharding import PartitionSpec as P

MESH = pl.DeviceIdType.MESH
BF16, F32 = jnp.bfloat16, jnp.float32
SEQ, RES, CH = 32, 128, 256
HALF, OUTC = 32, 128
ROWS, COLS = 16, 8
SEQ_ALL = SEQ * ROWS
OCT = 8
PIECE = OCT * HALF
NQ = 4
NC = 4
QL = HALF * RES // NQ
QC = HALF * RES // NC
SSTEP = 8
NT = (((1,), (1,)), ((), ()))

R_ROLES = ("sib", "xp", "dn", "up", "oa", "ob", "xdn", "xup", "xoa", "xob")
PIECES = ("own", "dn", "up", "xp", "o", "xdn", "xup", "xo")
PAIR = 2
SUB = 2
EARLY = 3
TRIGGER, TRIGGER_FROM = 'dn', 0
PARTS = (0, 1, 2, 3)
Z_FIRST = (3,)

ORDER = (
    ('e', (
        "r sib 0", "r sib 1", "r sib 2", "r xp 0", "r dn 0", "r up 0", "r xp 1", "r dn 1", "r up 1", "f xp 0",
        "T", "r xp 2", "r sib 3", "f dn 0", "f up 0", "f xp 1", "r dn 2", "r up 2", "r xp 3", "f dn 1",
        "f up 1", "r xdn 0", "r xup 0", "f xp 2", "f dn 2", "r oa 0", "f up 2", "f xp 3", "r up 3", "f xdn 0",
        "r dn 3", "r ob 0", "f xup 0", "f oa 0", "l dn 0", "l up 0", "f up 3", "r xdn 1", "r xup 1", "f dn 3",
        "f ob 0", "r oa 1", "r ob 1", "l xp 0", "f xdn 1", "r xdn 2", "r xup 2", "f xup 1", "l dn 1", "l up 1",
        "f oa 1", "f ob 1", "r oa 2", "r ob 2", "r xup 3", "r xoa 0", "r xob 0", "l xp 1", "f xdn 2", "r oa 3",
        "r ob 3", "r xdn 3", "f xup 2", "f oa 2", "f ob 2", "r xoa 1", "r xob 1", "f xup 3", "l o 0",
        "f xoa 0", "f xob 0",
    )),
    ('c', (
        (0, 1, 0),
    )),
    ('e', (
        "r xoa 2", "r xob 2", "l xup 0", "f oa 3", "f ob 3", "f xdn 3",
    )),
    ('c', (
        (1, 2, 0),
    )),
    ('e', (
        "f xoa 1", "r xoa 3", "f xob 1",
    )),
    ('c', (
        (0, 1, 1),
    )),
    ('e', (
        "r xob 3", "l xdn 0", "f xoa 2", "f xob 2",
    )),
    ('c', (
        (1, 2, 1),
    )),
    ('e', (
        "l o 1",
    )),
    ('c', (
        (0, 1, 2),
    )),
    ('e', (
        "f xoa 3",
    )),
    ('c', (
        (1, 2, 2),
    )),
    ('e', (
        "f xob 3", "l xdn 1",
    )),
    ('c', (
        (2, 3, 0),
    )),
    ('e', (
        "l xup 1",
    )),
    ('c', (
        (2, 3, 1),
    )),
    ('e', (
        "l xo 0",
    )),
    ('c', (
        (2, 3, 2), (0, 3, 3),
    )),
    ('e', (
        "l xo 1",
    )),
    ('c', (
        (3, 4, 0), (3, 4, 1), (3, 4, 2), (3, 4, 3),
    )),
)


def project(x_hbm, x_ref, x_s, scale_ref, wl_ref, wr_ref, z_ref):
    wt = jnp.concatenate([wl_ref[...], wr_ref[...]], axis=0).astype(F32) * scale_ref[...]
    hi = wt.astype(BF16)
    lo = (wt - hi.astype(F32)).astype(BF16)
    colsum = jnp.sum(hi.astype(F32) + lo.astype(F32), axis=1, keepdims=True)
    ones = jnp.ones((16, CH), BF16)
    lhs = jnp.concatenate([hi, lo, ones], axis=0)

    def chunk(k, carry):
        rows = pl.ds(k * SSTEP, SSTEP)
        pltpu.make_async_copy(x_hbm.at[rows], x_ref.at[rows], x_s.at[k]).wait()
        xc = x_ref[rows].reshape(SSTEP * RES, CH)
        p = lax.dot_general(lhs, xc, NT, preferred_element_type=F32)
        xf = xc.astype(F32)
        sq = xf * xf
        sqh = sq.astype(BF16)
        sql = (sq - sqh.astype(F32)).astype(BF16)
        s2 = lax.dot_general(ones, sqh, NT, preferred_element_type=F32) + lax.dot_general(
            ones, sql, NT, preferred_element_type=F32
        )
        mean = p[128:136] * (1.0 / CH)
        mh = mean.astype(BF16).astype(F32)
        ml = mean - mh
        var = (s2[0:8] * (1.0 / CH) - mh * mh) - ml * (2.0 * mh + ml)
        rstd = lax.rsqrt(jnp.maximum(var, 0.0) + 1e-05)
        y = (p[0:64] + p[64:128] - colsum * mean[0:1]) * rstd[0:1]
        for s in range(SSTEP):
            z_ref[k * SSTEP + s] = y[:, s * RES : (s + 1) * RES]
        return carry

    lax.fori_loop(0, SEQ // SSTEP, chunk, 0, unroll=True)


def kernel(
    x_hbm, scale_hbm, wl_hbm, wr_hbm, w_hbm, off_hbm, out_ref,
    x_ref, scale_ref, wl_ref, wr_ref, w_ref, off_ref,
    z_ref, zl_ref, yl_ref, lsend, lt, lf, rf, w2t, wf, ob, acc, outv,
    x_s, p_s, o_s, t_ss, t_rs, l_ss, l_rs, r_ss, r_rs, f_ss, f_rs,
):
    params = ((scale_hbm, scale_ref), (wl_hbm, wl_ref), (wr_hbm, wr_ref), (w_hbm, w_ref), (off_hbm, off_ref))
    params = [pltpu.make_async_copy(a, b, p_s.at[k]) for k, (a, b) in enumerate(params)]
    for d in params[:3]:
        d.start()
    for k in range(SEQ // SSTEP):
        rows = pl.ds(k * SSTEP, SSTEP)
        pltpu.make_async_copy(x_hbm.at[rows], x_ref.at[rows], x_s.at[k]).start()
    for d in params[3:]:
        d.start()

    r, c = lax.axis_index("row"), lax.axis_index("col")
    xl, z, h = r // 8, (r // 2) % 4, r % 2
    xh, y = c // 4, c % 4

    def row_of(xl_, z_, h_):
        return xl_ * 8 + lax.rem(z_ + 4, 4) * 2 + h_

    def col_of(xh_, y_):
        return xh_ * 4 + lax.rem(y_ + 4, 4)

    sib = (row_of(xl, z, 1 - h), c)
    r_dev = {"xp": (row_of(1 - xl, z, h), c), "up": (row_of(xl, z + 1, h), c), "dn": (row_of(xl, z - 1, h), c)}
    l_dev = {"xp": (r, col_of(1 - xh, y)), "up": (r, col_of(xh, y + 1)), "dn": (r, col_of(xh, y - 1))}

    barrier = pltpu.get_barrier_semaphore()
    owner = r // 2
    for dev in (sib, *r_dev.values(), *l_dev.values()):
        pl.semaphore_signal(barrier, inc=1, device_id=dev, device_id_type=MESH)
    for k in range(ROWS):

        @pl.when(jnp.logical_or(k != r, owner != c))
        def _():
            pl.semaphore_signal(barrier, inc=1, device_id=(k, owner), device_id_type=MESH)

    for d in params[:3]:
        d.wait()
    project(x_hbm, x_ref, x_s, scale_ref, wl_ref, wr_ref, z_ref)

    for a in range(HALF):
        yl_ref[a] = z_ref[:, a, :].astype(BF16)
    eye = (
        lax.broadcasted_iota(jnp.int32, (RES, RES), 0) == lax.broadcasted_iota(jnp.int32, (RES, RES), 1)
    ).astype(BF16)
    for t in range(8):
        b = jnp.concatenate([yl_ref[t + 8 * g] for g in range(4)], axis=0)
        zl_ref[:, t, :] = lax.dot_general(eye, b, NT, preferred_element_type=F32)
    lsend[...] = zl_ref[...].reshape(RES * 8, 128).astype(BF16)

    pl.semaphore_wait(barrier, jnp.where(owner == c, 22, 23))

    for k in range(ROWS):
        o = k
        to_row, to_col = 2 * c + o // COLS, o % COLS
        src = lsend.at[pl.ds(o * 64, 64)]
        mine = jnp.logical_and(to_row == r, to_col == c)

        @pl.when(mine)
        def _():
            pltpu.make_async_copy(src, lt.at[r], t_rs.at[r]).start()

        @pl.when(jnp.logical_not(mine))
        def _():
            pltpu.make_async_remote_copy(
                src, lt.at[r], t_ss.at[k], t_rs.at[r], device_id=(to_row, to_col), device_id_type=MESH
            ).start()

    for b in range(HALF):
        rf[pl.ds(pl.multiple_of(r * SEQ, SEQ), SEQ), pl.ds(b * RES, RES)] = z_ref[:, HALF + b, :].astype(BF16)

    def r_ref(q, xl_, z_, h_, half=None):
        rows = row_of(xl_, z_, h_) * SEQ
        n = SEQ
        if half is not None:
            rows, n = rows + half * (SEQ // 2), SEQ // 2
        return rf.at[pl.ds(pl.multiple_of(rows, n), n), pl.ds(q * QL, QL)]

    def r_block(q, role, h_):
        return {
            "own": lambda: r_ref(q, xl, z, h_),
            "xp": lambda: r_ref(q, 1 - xl, z, h_),
            "dn": lambda: r_ref(q, xl, z - 1, h_),
            "up": lambda: r_ref(q, xl, z + 1, h_),
            "oa": lambda: r_ref(q, xl, z + 2, h_, 0),
            "ob": lambda: r_ref(q, xl, z + 2, h_, 1),
            "xdn": lambda: r_ref(q, 1 - xl, z - 1, h_),
            "xup": lambda: r_ref(q, 1 - xl, z + 1, h_),
            "xoa": lambda: r_ref(q, 1 - xl, z + 2, h_, 0),
            "xob": lambda: r_ref(q, 1 - xl, z + 2, h_, 1),
        }[role]()

    def copy(src, sems, at, dev):
        return pltpu.make_async_remote_copy(
            src, src, sems[0].at[at], sems[1].at[at], device_id=dev, device_id_type=MESH
        )

    sends = []

    def r_send(q, role, src, dev):
        d = copy(src, (r_ss, r_rs), (q, R_ROLES.index(role)), dev)
        d.start()
        sends.append(d)

    def f_send(q, role):
        d = copy(r_block(q, role, h), (f_ss, f_rs), (q, R_ROLES.index(role)), sib)
        d.start()
        sends.append(d)

    def r_wait(q, role):
        ref = r_block(q, "own" if role == "sib" else role, 1 - h if role == "sib" else h)
        pltpu.make_async_copy(ref, ref, r_rs.at[q, R_ROLES.index(role)]).wait()

    def f_wait(q, role):
        ref = r_block(q, role, 1 - h)
        pltpu.make_async_copy(ref, ref, f_rs.at[q, R_ROLES.index(role)]).wait()

    def r_own(q):
        own = r_ref(q, xl, z, h)
        r_send(q, "xp", own, r_dev["xp"])
        r_send(q, "dn", own, r_dev["up"])
        r_send(q, "up", own, r_dev["dn"])
        r_send(q, "sib", own, sib)

    def r_event(role, q):
        r_wait(q, role)
        crossed = q not in Z_FIRST
        if role == "dn":
            r_send(q, "oa", r_ref(q, xl, z - 1, h, 0), r_dev["up"])
        elif role == "up":
            r_send(q, "ob", r_ref(q, xl, z + 1, h, 1), r_dev["dn"])
        elif role == "xp" and crossed:
            r_send(q, "xdn", r_block(q, "xp", h), r_dev["up"])
            r_send(q, "xup", r_block(q, "xp", h), r_dev["dn"])
        elif role == "xdn" and crossed:
            r_send(q, "xoa", r_ref(q, 1 - xl, z - 1, h, 0), r_dev["up"])
        elif role == "xup" and crossed:
            r_send(q, "xob", r_ref(q, 1 - xl, z + 1, h, 1), r_dev["dn"])
        if not crossed and role in ("dn", "up", "oa", "ob"):
            r_send(q, "x" + role, r_block(q, role, h), r_dev["xp"])
        if role == TRIGGER and later and q >= TRIGGER_FROM:
            r_own(later.pop(0))
        if role != "sib":
            f_send(q, role)

    asc = list(range(SUB))
    desc = asc[SUB // 2 :] + asc[: SUB // 2]

    def l_ref(role, k):
        n = PIECE // SUB
        return lf.at[pl.ds(PIECES.index(role) * PIECE + k * n, n)]

    def l_send(role, k, src, dev):
        at = (PIECES.index(role), k)
        d = pltpu.make_async_remote_copy(
            l_ref(src, k), l_ref(role, k), l_ss.at[at], l_rs.at[at], device_id=l_dev[dev], device_id_type=MESH
        )
        d.start()
        sends.append(d)

    def l_wait(role, k):
        ref = l_ref(role, k)
        pltpu.make_async_copy(ref, ref, l_rs.at[PIECES.index(role), k]).wait()

    def l_own():
        for k in range(ROWS):
            pltpu.make_async_copy(lt.at[k], lt.at[k], t_rs.at[k]).wait()
        v = jnp.concatenate([jnp.concatenate([lt[4 * g + k] for k in range(4)], axis=1) for g in range(4)], axis=0)
        w = jnp.dot(v, perm, preferred_element_type=F32)
        for g in range(4):
            u = [w[64 * g : 64 * (g + 1), 128 * k : 128 * (k + 1)].reshape(OCT, 8, 128) for k in range(4)]
            lf[pl.ds(0, PIECE), pl.ds(g * 128, 128)] = jnp.concatenate(u, axis=1).reshape(PIECE, 128).astype(BF16)
        for i in range(SUB):
            l_send("xp", (asc, desc)[i % 2][i // 2], "own", "xp")
            l_send("dn", asc[i], "own", "up")
            l_send("up", desc[i], "own", "dn")

    def l_event(role, k):
        l_wait(role, k)
        if role == "dn" and k < SUB // 2:
            l_send("o", k, "dn", "up")
        elif role == "up" and k >= SUB // 2:
            l_send("o", k, "up", "dn")
        elif role == "xp":
            l_send("xdn", k, "xp", "up")
            l_send("xup", k, "xp", "dn")
        elif role == "o":
            l_send("xo", k, "o", "xp")

    def event(name):
        if name == "T":
            l_own()
            return
        kind, role, k = name.split()
        {"r": r_event, "l": l_event, "f": lambda role, q: f_wait(q, role)}[kind](role, int(k))


    def piece_of(k):
        flip = jnp.logical_or(k == 3, k >= 5)
        dy = jnp.where(jnp.logical_or(k == 1, k == 5), 3, jnp.where(jnp.logical_or(k == 2, k == 6), 1, 0))
        dy = jnp.where(jnp.logical_or(k == 4, k == 7), 2, dy)
        return col_of(jnp.where(flip, 1 - xh, xh), y + dy)

    nb = QC // RES

    rows = PAIR * OCT

    def outer(p, q, slot):
        lhs = lf[pl.ds(pl.multiple_of(p * PAIR * PIECE, PIECE), PAIR * PIECE)]
        o = jnp.dot(lhs, rf[:, pl.ds(pl.multiple_of(q * QC, QC), QC)], preferred_element_type=F32).astype(BF16)
        ob[slot] = jnp.concatenate(
            [
                jnp.concatenate([o[i * HALF : (i + 1) * HALF, b * RES : (b + 1) * RES] for b in range(nb)], axis=0)
                for i in range(rows)
            ],
            axis=1,
        )

    def final(p, q, slot):
        w = w2t[:, pl.ds(pl.multiple_of(q * nb * HALF, nb * HALF), nb * HALF)]
        acc[p] += jnp.dot(w, ob[slot], preferred_element_type=F32)

    def out_copy(k):
        rows = pl.ds(piece_of(k) * OCT, OCT)
        return pltpu.make_async_copy(outv.at[rows], out_ref.at[rows], o_s.at[k])

    def finish(p):
        for k in range(PAIR):
            m = piece_of(p * PAIR + k)
            for i in range(OCT):
                at = (k * OCT + i) * RES
                t = acc[p, :, at : at + RES].T
                outv[m * OCT + i] = (t * (1.0 / SEQ_ALL) + off).astype(BF16)
            out_copy(p * PAIR + k).start()

    def run(first, end, q, before, q_before):
        def step(k, before, done):
            pk, pq, slot = before
            if pk is not None:
                final(pk, pq, slot)
            outer(k, q, 1 - slot)
            if done:
                finish(pk)
            return k, jnp.int32(q), 1 - slot

        before = step(jnp.int32(first), before, q_before == NC - 1)
        if first + 1 < end:
            before = lax.fori_loop(first + 1, end, lambda k, b: step(k, b, q == NC - 1), before)
        return before

    later = list(PARTS[EARLY:])
    for q in PARTS[:EARLY]:
        r_own(q)

    acc[...] = jnp.zeros_like(acc)
    for d in params[3:]:
        d.wait()
    off = off_ref[...]
    i0 = lax.broadcasted_iota(jnp.int32, (512, 512), 0)
    i1 = lax.broadcasted_iota(jnp.int32, (512, 512), 1)
    to = ((i0 // 32) % 4) * 128 + (i0 // 128) * 32 + i0 % 32
    perm = (to == i1).astype(BF16)
    wf[...] = w_ref[...].astype(F32).reshape(HALF, HALF, OUTC)
    for t in range(8):
        blk = jnp.concatenate([wf[:, 4 * t + k, :] for k in range(4)], axis=0)
        w2t[:, pl.ds(t * 128, 128)] = blk.T.astype(BF16)

    before, q_before = (None, jnp.int32(0), jnp.int32(0)), None
    for kind, what in ORDER:
        for x in what:
            if kind == "e":
                event(x)
            else:
                before = run(*x, tuple(jnp.int32(v) if v is not None else v for v in before), q_before)
                q_before = x[2]
    final(*before)
    finish(before[0])
    for k in range(COLS):
        out_copy(k).wait()

    for k in range(ROWS):
        o = k
        mine = jnp.logical_and(2 * c + o // COLS == r, o % COLS == c)

        @pl.when(jnp.logical_not(mine))
        def _():
            src = lsend.at[pl.ds(o * 64, 64)]
            pltpu.make_async_copy(src, src, t_ss.at[k]).wait()

    for d in sends:
        d.wait_send()


def place(src, dst, held, sems):
    parts = [pl.ds(k * OCT, OCT) for k in range(COLS)]
    ins = [pltpu.make_async_copy(src.at[p], held.at[p], sems.at[0, k]) for k, p in enumerate(parts)]
    outs = [pltpu.make_async_copy(held.at[p], dst.at[p], sems.at[1, k]) for k, p in enumerate(parts)]
    for d in ins:
        d.start()
    for d, e in zip(ins, outs):
        d.wait()
        e.start()
    for e in outs:
        e.wait()


def body(x, scale, wl, wr, w, off):
    dma = pltpu.SemaphoreType.DMA
    out = pl.pallas_call(
        kernel,
        out_shape=jax.ShapeDtypeStruct((64, RES, OUTC), BF16),
        in_specs=[pl.BlockSpec(memory_space=pltpu.HBM)] * 6,
        out_specs=pl.BlockSpec(memory_space=pltpu.HBM),
        scratch_shapes=[
            pltpu.VMEM((SEQ, RES, CH), BF16),
            pltpu.VMEM((1, CH), F32),
            pltpu.VMEM((HALF, CH), BF16),
            pltpu.VMEM((HALF, CH), BF16),
            pltpu.VMEM((HALF * HALF, OUTC), BF16),
            pltpu.VMEM((1, OUTC), F32),
            pltpu.VMEM((SEQ, 64, RES), F32),
            pltpu.VMEM((RES, 8, 128), F32),
            pltpu.VMEM((HALF, SEQ, RES), BF16),
            pltpu.VMEM((RES * 8, 128), BF16),
            pltpu.VMEM((ROWS, 64, 128), BF16),
            pltpu.VMEM((COLS * PIECE, SEQ_ALL), BF16),
            pltpu.VMEM((SEQ_ALL, HALF * RES), BF16),
            pltpu.VMEM((OUTC, HALF * HALF), BF16),
            pltpu.VMEM((HALF, HALF, OUTC), F32),
            pltpu.VMEM((2, QC // RES * HALF, PAIR * OCT * RES), BF16),
            pltpu.VMEM((COLS // PAIR, OUTC, PAIR * OCT * RES), F32),
            pltpu.VMEM((64, RES, OUTC), BF16),
            dma((SEQ // SSTEP,)), dma((5,)), dma((COLS,)),
            dma((ROWS,)), dma((ROWS,)),
            dma((COLS, SUB)), dma((COLS, SUB)),
            dma((NQ, len(R_ROLES))), dma((NQ, len(R_ROLES))),
            dma((NQ, len(R_ROLES))), dma((NQ, len(R_ROLES))),
        ],
        compiler_params=pltpu.CompilerParams(
            collective_id=0, has_side_effects=True, vmem_limit_bytes=62 * 2**20
        ),
        cost_estimate=pl.CostEstimate(flops=11 * 10**9, bytes_accessed=5 * 10**6, transcendentals=4096),
        name="outer_product_mean",
    )(x, scale.reshape(1, CH), wl.T, wr.T, w, off.reshape(1, OUTC))
    return pl.pallas_call(
        place,
        out_shape=jax.ShapeDtypeStruct(out.shape, out.dtype),
        in_specs=[pl.BlockSpec(memory_space=pltpu.HBM)],
        out_specs=pl.BlockSpec(memory_space=pltpu.HBM),
        scratch_shapes=[pltpu.VMEM((64, RES, OUTC), BF16), dma((2, COLS))],
        compiler_params=pltpu.CompilerParams(vmem_limit_bytes=62 * 2**20),
        name="place",
    )(out)


def solution(mesh):
    in_specs = (P("row", "col", None), P(), P(), P(), P(), P())
    return jax.shard_map(body, mesh=mesh, in_specs=in_specs, out_specs=P("row", "col", None), check_vma=False)
```
